512 devices in a mesh: row: 64 (over z_hi, y, x), chan: 8 (over z_lo, core).
Axes of the slice: x: 4, y: 8, z: 8 (z_hi: 2, z_lo: 4; z = z_hi * 4 + z_lo), core: 2. Of those that a mesh axis runs over, the one named last changes fastest.
Arguments:
- pair_in: bfloat16 [128, 512, 512], P('chan', 'row'), may hold values from -200 to 200, as said below
- token_mask: int32 [512], replicated, may hold values 0 or 1
- in_gain: bfloat16 [128], P('chan'), may hold values from 0.5 to 1.5
- in_bias: bfloat16 [128], P('chan'), may hold values from -3 to 3
- in_weight: bfloat16 [4, 128, 128], P(None, None, 'chan'), may hold values from -0.5 to 0.5
- out_gain: float32 [128], P('chan'), may hold values from 0.5 to 1.5
- out_bias: float32 [128], P('chan'), may hold values from -3 to 3
- out_weight: bfloat16 [128, 128], replicated, may hold values from -0.5 to 0.5
- gate_weight: bfloat16 [128, 128], P(None, 'chan'), may hold values from -0.5 to 0.5
Outputs:
- result: bfloat16 [128, 512, 512], P('chan', 'row')
The draws below stay inside these ranges and needn't reach their ends.
Inputs may be any that keep to these rules, and one draw needn't show every extreme that they name: `pair_in`: pair features.
All inputs are finite; a program needn't handle non-finite values.
Results may differ from the reference program's by a relative error of at most 0.0053.
Values may be sent and summed in bfloat16 or wider, within the bound.
A program may use at most 64 MiB of HBM per device.

```python
import math
import jax
import jax.numpy as jnp
from jax import lax

C = 128
CH = 128
TOKENS = 512


def draw_pair_in(key, part):
    key = jax.random.fold_in(key, 11)
    first, second, third, fourth = jax.random.split(key, 4)
    channel = jnp.arange(C, dtype=jnp.float32) / max(C - 1, 1)
    base = jax.random.truncated_normal(first, -4.0, 4.0, (C, TOKENS, TOKENS), jnp.float32)
    rise = jnp.exp(math.log(3.0) * channel)
    channel_scale = rise[:, None, None] * jnp.exp(jax.random.uniform(second, (C, 1, 1), jnp.float32, 0.0, math.log(3.0)))
    channel_scale = channel_scale / 3.0
    position_scale = jnp.exp(jax.random.uniform(third, (1, TOKENS, TOKENS), jnp.float32, 0.0, math.log(10.0)))
    offset = jax.random.uniform(fourth, (C, 1, 1), jnp.float32, -1.0, 1.0)
    values = (base * channel_scale + offset) * position_scale
    return values.astype(jnp.bfloat16)


def touch_ends(entries, key, least, largest):
    longest = entries.shape.index(max(entries.shape))
    spots = []
    for shift in (0, 1):
        where = [jax.random.randint(jax.random.fold_in(key, axis), (), 0, length) for axis, length in enumerate(entries.shape)]
        where[longest] = (where[longest] + shift) % entries.shape[longest]
        spots.append(tuple(where))
    return entries.at[spots[0]].set(least).at[spots[1]].set(largest)


def levels(stream_key, dims, shards, low, high):
    level = 1.0
    for position, parts in shards:
        steps = jax.random.uniform(jax.random.fold_in(jax.random.fold_in(stream_key, 6), position), (parts,), jnp.float32, low / len(shards), high / len(shards))
        level = level * jnp.repeat(jnp.exp(steps), dims[position] // parts).reshape((-1,) + (1,) * (len(dims) - 1 - position))
    return level


def bell_draw(own_key, extent, scale, most, cuts=(), kind=jnp.bfloat16):
    drawn = scale * jax.random.normal(own_key, extent, jnp.float32)
    if cuts:
        drawn = drawn * levels(own_key, extent, cuts, -0.22, 0.18)
    return jnp.clip(drawn, -most, most).astype(kind)


def setup_inputs(seed: int = 0) -> dict:
    key_of = jax.random.split(jax.random.key(seed), 10)
    pair_in = draw_pair_in(jax.random.fold_in(key_of[9], 71), 0)
    token_mask = touch_ends((jax.random.randint(key_of[1], (TOKENS,), 0, 8) < 7).astype(jnp.int32), jax.random.fold_in(key_of[1], 1), 0, 1)
    in_gain = jnp.clip(0.5 + 1.0 * jax.random.uniform(key_of[2], (C,), jnp.float32) ** levels(key_of[2], (C,), ((0, 8),), -0.2, 0.2), 0.5, 1.5).astype(jnp.bfloat16)
    in_bias = bell_draw(key_of[3], (C,), 0.5, 3.0, ((0, 8),))
    in_weight = bell_draw(key_of[4], (4, C, CH), C ** -0.5, 0.5, ((2, 8),))
    out_gain = jnp.clip(0.5 + 1.0 * jax.random.uniform(key_of[5], (CH,), jnp.float32) ** levels(key_of[5], (CH,), ((0, 8),), -0.2, 0.2), 0.5, 1.5)
    out_bias = bell_draw(key_of[6], (CH,), 0.5, 3.0, ((0, 8),), jnp.float32)
    out_weight = bell_draw(key_of[7], (CH, C), CH ** -0.5, 0.5)
    gate_weight = bell_draw(key_of[8], (C, C), C ** -0.5, 0.5, ((1, 8),))
    return {"pair_in": pair_in, "token_mask": token_mask, "in_gain": in_gain, "in_bias": in_bias, "in_weight": in_weight, "out_gain": out_gain, "out_bias": out_bias, "out_weight": out_weight, "gate_weight": gate_weight}


epsilon = 1e-05

def layer_norm(values, gain, bias):
    mean = lax.optimization_barrier(jnp.mean(values, axis=0))
    center = values - mean
    spread = lax.optimization_barrier(jnp.mean(center * center, axis=0))
    return center * lax.rsqrt(spread + epsilon) * gain[:, None, None] + bias[:, None, None]

def reference(pair_in, token_mask, in_gain, in_bias, in_weight, out_gain, out_bias, out_weight, gate_weight):
    high = lax.Precision.HIGHEST
    normed = layer_norm(pair_in.astype(jnp.float32), in_gain.astype(jnp.float32), in_bias.astype(jnp.float32)).astype(jnp.bfloat16)
    normed_wide = normed.astype(jnp.float32)
    proj = jnp.einsum('pch,cik->phik', in_weight.astype(jnp.float32), normed_wide, precision=high)
    valid = token_mask.astype(jnp.float32)
    pair_mask = valid[:, None] * valid[None, :]
    left = (jax.nn.sigmoid(proj[1]) * proj[0] * pair_mask).astype(jnp.bfloat16)
    right = (jax.nn.sigmoid(proj[3]) * proj[2] * pair_mask).astype(jnp.bfloat16)
    triangle = jnp.einsum('cik,cjk->cij', left.astype(jnp.float32), right.astype(jnp.float32), precision=high)
    hidden_norm = layer_norm(triangle, out_gain, out_bias).astype(jnp.bfloat16)
    gate = jax.nn.sigmoid(jnp.einsum('cd,cij->dij', gate_weight.astype(jnp.float32), normed_wide, precision=high))
    mixed = jnp.einsum('hd,hij->dij', out_weight.astype(jnp.float32), hidden_norm.astype(jnp.float32), precision=high)
    return (mixed * gate).astype(jnp.bfloat16)
```

```python
import jax
import jax.numpy as jnp
from jax import lax
from jax.experimental import pallas as pl
from jax.experimental.pallas import tpu as pltpu
from jax.sharding import PartitionSpec as P

MESH = pl.DeviceIdType.MESH
EPS = 1e-05
NZH, NY, NX, NZL, NC = 2, 8, 4, 4, 2
NCH = NZL * NC
T = 4
KC = 128
F32 = jnp.float32
BF16 = jnp.bfloat16


def dot(a, b):
    return jnp.dot(a, b, preferred_element_type=F32)


def column(vec):
    n = vec.shape[1]
    a = lax.broadcasted_iota(jnp.int32, (n, n), 0)
    b = lax.broadcasted_iota(jnp.int32, (n, n), 1)
    return jnp.sum(jnp.where(a == b, jnp.broadcast_to(vec, (n, n)), 0.0), axis=1, keepdims=True)


def kernel(
    pair, tm_s, tm_v, ig, ib, w, og, ob, wo, gw,
    out,
    xf, xb, pm, gb, lr_f, lb, rb, acc, e_f, es, er, fs, fr, gate, perm, wot, o_f,
    xs_sem, xr_sem, ps_sem, pr_sem, ls_sem, lr_sem, rs_sem, rr_sem, es_sem, er_sem, fs_sem, fr_sem,
):
    row = lax.axis_index("row")
    chan = lax.axis_index("chan")
    zh = lax.div(row, NY * NX)
    y = lax.rem(lax.div(row, NX), NY)
    x = lax.rem(row, NX)
    zl = lax.div(chan, NC)
    core = lax.rem(chan, NC)
    me_m = zh * NX + x

    def row_of(zh_, y_, x_):
        return (zh_ * NY + y_) * NX + x_

    def yrow(d):
        return row_of(zh, lax.rem(y + (NY + d), NY), x)

    def xrow(d):
        return row_of(zh, y, lax.rem(x + (NX + d), NX))

    row_z = row_of(1 - zh, y, x)
    row_f = row_of(lax.div(chan, NX), y, lax.rem(chan, NX))
    self_f = me_m == chan
    sibling = zl * NC + (1 - core)

    bar = pltpu.get_barrier_semaphore()

    def greet(r, c):
        pl.semaphore_signal(bar, inc=1, device_id=(r, c), device_id_type=MESH)

    for s in range(1, NCH):
        greet(row, lax.rem(chan + s, NCH))
    for r in (yrow(1), yrow(-1), xrow(1), xrow(-1), row_z):
        greet(r, chan)
    for s in range(1, NCH):
        m = lax.rem(me_m + s, NCH)
        greet(row_of(lax.div(m, NX), y, lax.rem(m, NX)), me_m)

    @pl.when(jnp.logical_not(self_f))
    def _():
        greet(row, me_m)

    sends = []

    def send(src, dst, ssem, rsem, r, c):
        copy = pltpu.make_async_remote_copy(
            src_ref=src, dst_ref=dst, send_sem=ssem, recv_sem=rsem,
            device_id=(r, c), device_id_type=MESH,
        )
        copy.start()
        sends.append(copy)

    def arrived(ref, ssem, rsem):
        pltpu.make_async_remote_copy(
            src_ref=ref, dst_ref=ref, send_sem=ssem, recv_sem=rsem,
            device_id=(row, sibling), device_id_type=MESH,
        ).wait_recv()

    for t in range(T):
        xf[t] = pair[:, :, t * KC:(t + 1) * KC].astype(F32).reshape(128, KC)
        for r in range(8):
            xb[t, chan, r] = xf[t, pl.ds(r, 16, stride=8), :].astype(BF16)
    lane16 = lax.broadcasted_iota(jnp.int32, (16, 128), 1)
    cols = [column(v[...].astype(F32)) for v in (ig, ib, og, ob)]
    block = jnp.zeros((16, 128), F32)
    for n, col in enumerate(cols):
        block = jnp.where(lane16 == n, jnp.broadcast_to(col, (16, 128)), block)
    pm[chan] = block

    pl.semaphore_wait(bar, jnp.where(self_f, 2 * NCH + 3, 2 * NCH + 4))

    for s in range(1, NCH):
        send(pm.at[chan], pm.at[chan], ps_sem.at[s], pr_sem.at[chan], row, lax.rem(chan + s, NCH))
    for t in range(T):
        for d in range(1, NZL):
            c = lax.rem(zl + d, NZL) * NC + core
            send(xb.at[t, chan], xb.at[t, chan], xs_sem.at[t, d], xr_sem.at[t, chan], row, c)
        send(xb.at[t, chan], xb.at[t, chan], xs_sem.at[t, 0], xr_sem.at[t, chan], row, sibling)

    ki = lax.broadcasted_iota(jnp.int32, (512, 512), 0)
    ni = lax.broadcasted_iota(jnp.int32, (512, 512), 1)
    kx, ky, kp, k8 = ki >> 7, (ki >> 4) & 7, (ki >> 3) & 1, ki & 7
    want = (kp << 8) | (ky << 5) | (kx << 3) | k8
    perm[...] = jnp.where(want == ni, 1.0, 0.0).astype(BF16)
    eye_a = lax.broadcasted_iota(jnp.int32, (128, 128), 0)
    eye_b = lax.broadcasted_iota(jnp.int32, (128, 128), 1)
    eye = jnp.where(eye_a == eye_b, 1.0, 0.0).astype(BF16)
    turned = lax.dot_general(eye, wo[...], (((1,), (1,)), ((), ())), preferred_element_type=F32).astype(BF16)
    ha = lax.broadcasted_iota(jnp.int32, (128, 64), 0)
    hb = lax.broadcasted_iota(jnp.int32, (128, 64), 1)
    for par in range(2):
        pick = jnp.where(ha == 2 * hb + par, 1.0, 0.0).astype(BF16)
        wot[par * 128:(par + 1) * 128, :] = dot(turned, pick).astype(BF16)

    wt = jnp.concatenate([w[...].reshape(64, 128), gw[...]], axis=0)
    for s in range(1, NCH):
        c = lax.rem(chan + s, NCH)
        arrived(pm.at[c], ps_sem.at[s], pr_sem.at[c])
    pmv = pm[...].reshape(128, 128)
    gb[0] = jnp.broadcast_to(pmv[:, 0:1], (128, 128))
    gb[1] = jnp.broadcast_to(pmv[:, 1:2], (128, 128))
    row_valid = [tm_s[row * 8 + r].astype(F32) for r in range(8)]

    def gather_in(t):
        for d in range(1, NZL):
            c = lax.rem(zl + d, NZL) * NC + core
            arrived(xb.at[t, c], xs_sem.at[t, 0], xr_sem.at[t, c])
            send(xb.at[t, c], xb.at[t, c], xs_sem.at[t, 3 + d], xr_sem.at[t, c], row, sibling)
        for d in range(NZL):
            c = lax.rem(zl + d, NZL) * NC + (1 - core)
            arrived(xb.at[t, c], xs_sem.at[t, 0], xr_sem.at[t, c])

    def project(t):
        pieces = []
        gain = gb[0]
        bias = gb[1]
        for r in range(8):
            v = xb[t, :, r].astype(F32).reshape(128, KC)
            mean = jnp.sum(v, axis=0, keepdims=True) * (1.0 / 128)
            center = v - mean
            spread = jnp.sum(center * center, axis=0, keepdims=True) * (1.0 / 128)
            pieces.append((center * lax.rsqrt(spread + EPS) * gain + bias).astype(BF16))
        normed = jnp.concatenate(pieces, axis=1)
        proj = dot(wt, normed)
        col_valid = tm_v[:, t * KC:(t + 1) * KC].astype(F32)
        mask = jnp.concatenate([col_valid * s for s in row_valid], axis=1)
        left = jax.nn.sigmoid(proj[16:32]) * proj[0:16] * mask
        right = jax.nn.sigmoid(proj[48:64]) * proj[32:48] * mask
        g = jax.nn.sigmoid(proj[64:80])
        for r in range(8):
            lr_f[0, pl.ds(r, 16, stride=8), :] = left[:, r * KC:(r + 1) * KC]
            lr_f[1, pl.ds(r, 16, stride=8), :] = right[:, r * KC:(r + 1) * KC]
            gate[r, :, t * KC:(t + 1) * KC] = g[:, r * KC:(r + 1) * KC]
        lb[t, me_m] = lr_f[0].astype(BF16)
        rb[t, y] = lr_f[1].astype(BF16)

    def lslot(far, d):
        return (1 - zh if far else zh) * NX + lax.rem(x + (NX + d), NX)

    def rslot(d):
        return lax.rem(y + (NY + d), NY)

    def send_l(t, n, slot, r):
        send(lb.at[t, slot], lb.at[t, slot], ls_sem.at[t, n], lr_sem.at[t, slot], r, chan)

    def send_r(t, n, slot, r):
        send(rb.at[t, slot], rb.at[t, slot], rs_sem.at[t, n], rr_sem.at[t, slot], r, chan)

    def got_l(t, slot):
        arrived(lb.at[t, slot], ls_sem.at[t, 0], lr_sem.at[t, slot])

    def got_r(t, slot):
        arrived(rb.at[t, slot], rs_sem.at[t, 0], rr_sem.at[t, slot])

    def step1(t):
        send_l(t, 0, me_m, row_z)
        send_r(t, 0, y, yrow(1))
        send_r(t, 1, y, yrow(-1))
        send_l(t, 1, me_m, xrow(1))
        send_l(t, 2, me_m, xrow(-1))

    def step2(t):
        got_r(t, rslot(-1))
        send_r(t, 2, rslot(-1), yrow(1))
        got_r(t, rslot(1))
        send_r(t, 3, rslot(1), yrow(-1))
        got_l(t, lslot(False, -1))
        got_l(t, lslot(False, 1))
        if t % 2 == 0:
            send_l(t, 3, lslot(False, -1), xrow(1))
        else:
            send_l(t, 3, lslot(False, 1), xrow(-1))
        got_l(t, lslot(True, 0))
        send_l(t, 4, lslot(True, 0), xrow(1))
        send_l(t, 5, lslot(True, 0), xrow(-1))

    def step3(t):
        got_r(t, rslot(-2))
        send_r(t, 4, rslot(-2), yrow(1))
        got_r(t, rslot(2))
        send_r(t, 5, rslot(2), yrow(-1))
        got_l(t, lslot(True, -1))
        got_l(t, lslot(True, 1))
        if t % 2 == 0:
            send_l(t, 6, lslot(True, 1), xrow(-1))
        else:
            send_l(t, 6, lslot(True, -1), xrow(1))

    def step4(t):
        got_r(t, rslot(-3))
        got_r(t, rslot(3))
        if t % 2 == 0:
            send_r(t, 6, rslot(-3), yrow(1))
        else:
            send_r(t, 6, rslot(3), yrow(-1))

    def step5(t):
        got_l(t, lslot(False, 2))
        got_l(t, lslot(True, 2))
        got_r(t, rslot(4))
        for h in range(8):
            a = lb[t, :, 16 * h:16 * h + 16, :].reshape(128, KC)
            b = rb[t, :, 16 * h:16 * h + 16, :].reshape(128, KC)
            part = lax.dot_general(a, b, (((1,), (1,)), ((), ())), preferred_element_type=F32)
            if t == 0:
                acc[h] = part
            else:
                acc[h] += part

    for wave in range(T + 4):
        if wave < T:
            gather_in(wave)
            project(wave)
            step1(wave)
        for back, step in ((4, step5), (3, step4), (2, step3), (1, step2)):
            if 0 <= wave - back < T:
                step(wave - back)

    lane = lax.broadcasted_iota(jnp.int32, (1, 128), 1)
    even = ((lane >> 3) & 1) == 0

    for h in range(8):
        o = acc[h].reshape(8, 2, 8, 128)
        own = jnp.where(even, o[:, 0].reshape(64, 128), o[:, 1].reshape(64, 128))
        e_f[pl.ds(h, 64, stride=8), :] = own
    es[...] = e_f[...].astype(BF16).reshape(8, 64, 128)
    for s in range(1, NCH):
        c = lax.rem(chan + s, NCH)
        send(es.at[c], er.at[chan], es_sem.at[s], er_sem.at[chan], row, c)
    er[chan] = es[chan]
    for s in range(1, NCH):
        c = lax.rem(chan + s, NCH)
        arrived(er.at[c], es_sem.at[s], er_sem.at[c])

    tri = er[...].astype(F32).reshape(8, 8, 8, 128)

    def across(v):
        return v + jnp.where(even, pltpu.roll(v, 120, 1), pltpu.roll(v, 8, 1))

    mean = across(jnp.sum(jnp.sum(tri, axis=0), axis=1)) * (1.0 / 128)
    center = tri - mean[None, :, None, :]
    spread = across(jnp.sum(jnp.sum(center * center, axis=0), axis=1)) * (1.0 / 128)
    inverse = lax.rsqrt(spread + EPS)
    e_f[0:128, :] = pmv
    g_e = e_f[pl.ds(0, 64, stride=2), :]
    g_o = e_f[pl.ds(1, 64, stride=2), :]
    gain = jnp.where(even, g_e[:, 2:3], g_o[:, 2:3])
    bias = jnp.where(even, g_e[:, 3:4], g_o[:, 3:4])
    hidden = jnp.concatenate(
        [
            (center[:, r].reshape(64, 128) * inverse[r:r + 1] * gain + bias).astype(BF16)
            for r in range(8)
        ],
        axis=1,
    )
    both = dot(wot[...], hidden)
    for q in range(4):
        a0 = both[0:128, 256 * q:256 * q + 128]
        a1 = both[0:128, 256 * q + 128:256 * q + 256]
        b0 = both[128:256, 256 * q:256 * q + 128]
        b1 = both[128:256, 256 * q + 128:256 * q + 256]
        mixed = jnp.where(even, a0 + pltpu.roll(b0, 120, 1), b1 + pltpu.roll(a1, 8, 1))
        fs[:, q] = mixed.astype(BF16).reshape(8, 16, 128)

    def f_copy():
        return pltpu.make_async_remote_copy(
            src_ref=fs.at[chan], dst_ref=fr.at[me_m], send_sem=fs_sem.at[0], recv_sem=fr_sem.at[me_m],
            device_id=(row_f, chan), device_id_type=MESH,
        )

    for s in range(1, NCH):
        c = lax.rem(chan + s, NCH)
        send(fs.at[c], fr.at[me_m], fs_sem.at[s], fr_sem.at[me_m], row_f, c)

    @pl.when(jnp.logical_not(self_f))
    def _():
        f_copy().start()

    @pl.when(self_f)
    def _():
        fr[me_m] = fs[chan]

    for s in range(1, NCH):
        m = lax.rem(me_m + s, NCH)
        arrived(fr.at[m], fs_sem.at[s], fr_sem.at[m])

    @pl.when(jnp.logical_not(self_f))
    def _():
        arrived(fr.at[me_m], fs_sem.at[0], fr_sem.at[me_m])

    for z in range(NZH):
        got = jnp.concatenate([fr[z * NX + i].reshape(64, 128) for i in range(NX)], axis=1)
        o = dot(got, perm[...])
        for q in range(4):
            for par in range(2):
                r = 2 * q + par
                val = o[16 * q:16 * q + 16, 256 * par:256 * par + 256] * gate[r, :, 256 * z:256 * z + 256]
                for half in range(2):
                    o_f[2 * z + half, pl.ds(r, 16, stride=8), :] = val[:, 128 * half:128 * half + 128]
    for n in range(4):
        out[:, :, 128 * n:128 * n + 128] = o_f[n].reshape(16, 8, 128).astype(BF16)

    for copy in sends:
        copy.wait_send()

    @pl.when(jnp.logical_not(self_f))
    def _():
        f_copy().wait_send()


def body(pair_in, token_mask, in_gain, in_bias, in_weight, out_gain, out_bias, out_weight, gate_weight):
    vm = pl.BlockSpec(memory_space=pltpu.VMEM)
    sm = pl.BlockSpec(memory_space=pltpu.SMEM)
    dma = pltpu.SemaphoreType.DMA
    return pl.pallas_call(
        kernel,
        out_shape=jax.ShapeDtypeStruct((16, 8, 512), BF16),
        in_specs=[vm, sm] + [vm] * 8,
        out_specs=vm,
        scratch_shapes=[
            pltpu.VMEM((T, 128, KC), F32),
            pltpu.VMEM((T, NCH, 8, 16, KC), BF16),
            pltpu.VMEM((NCH, 16, 128), F32),
            pltpu.VMEM((2, 128, 128), F32),
            pltpu.VMEM((2, 128, KC), F32),
            pltpu.VMEM((T, 8, 128, KC), BF16),
            pltpu.VMEM((T, 8, 128, KC), BF16),
            pltpu.VMEM((8, 128, 128), F32),
            pltpu.VMEM((512, 128), F32),
            pltpu.VMEM((8, 64, 128), BF16),
            pltpu.VMEM((8, 64, 128), BF16),
            pltpu.VMEM((8, 4, 16, 128), BF16),
            pltpu.VMEM((8, 4, 16, 128), BF16),
            pltpu.VMEM((8, 16, 512), F32),
            pltpu.VMEM((512, 512), BF16),
            pltpu.VMEM((256, 64), BF16),
            pltpu.VMEM((4, 128, 128), F32),
            dma((T, 7)), dma((T, NCH)),
            dma((NCH,)), dma((NCH,)),
            dma((T, 7)), dma((T, 8)),
            dma((T, 7)), dma((T, 8)),
            dma((NCH,)), dma((NCH,)),
            dma((NCH,)), dma((NCH,)),
        ],
        compiler_params=pltpu.CompilerParams(
            collective_id=0, has_side_effects=True, vmem_limit_bytes=48 * 1024 * 1024
        ),
    )(
        pair_in,
        token_mask,
        token_mask.reshape(1, 512),
        in_gain.reshape(1, 16),
        in_bias.reshape(1, 16),
        jnp.transpose(in_weight, (0, 2, 1)),
        out_gain.reshape(1, 16),
        out_bias.reshape(1, 16),
        out_weight,
        gate_weight.T,
    )


def solution(mesh):
    return jax.shard_map(
        body,
        mesh=mesh,
        in_specs=(
            P("chan", "row", None),
            P(),
            P("chan"),
            P("chan"),
            P(None, None, "chan"),
            P("chan"),
            P("chan"),
            P(),
            P(None, "chan"),
        ),
        out_specs=P("chan", "row", None),
        check_vma=False,
    )
```

```python
import jax
import jax.numpy as jnp
from jax import lax
from jax.experimental import pallas as pl
from jax.experimental.pallas import tpu as pltpu
from jax.sharding import PartitionSpec as P

MESH = pl.DeviceIdType.MESH
EPS = 1e-05
NZH, NY, NX, NZL, NC = 2, 8, 4, 4, 2
NCH = NZL * NC
T = 4
KC = 128
AHEAD = 2
F32 = jnp.float32
BF16 = jnp.bfloat16


def dot(a, b):
    return jnp.dot(a, b, preferred_element_type=F32)


def column(vec):
    n = vec.shape[1]
    a = lax.broadcasted_iota(jnp.int32, (n, n), 0)
    b = lax.broadcasted_iota(jnp.int32, (n, n), 1)
    return jnp.sum(jnp.where(a == b, jnp.broadcast_to(vec, (n, n)), 0.0), axis=1, keepdims=True)


def kernel(
    tm_s, *refs,
):
    ins, (out, *vins), (sem_in, *rest) = refs[:9], refs[9:19], refs[19:]
    run(tm_s, ins, out, vins, sem_in, *rest)


def run(
    tm_s, ins, out, vins, sem_in,
    xf, xb, pm, gb, lr_f, lb, rb, acc, e_f, es, er, fs, fr, gate, perm, wot, o_f,
    xs_sem, xr_sem, ps_sem, pr_sem, ls_sem, lr_sem, rs_sem, rr_sem, es_sem, er_sem, fs_sem, fr_sem,
):
    loads = [pltpu.make_async_copy(a, b, sem_in.at[n]) for n, (a, b) in enumerate(zip(ins, vins))]
    for load in loads:
        load.start()
    pair, tm_v, ig, ib, w, og, ob, wo, gw = vins
    row = lax.axis_index("row")
    chan = lax.axis_index("chan")
    zh = lax.div(row, NY * NX)
    y = lax.rem(lax.div(row, NX), NY)
    x = lax.rem(row, NX)
    zl = lax.div(chan, NC)
    core = lax.rem(chan, NC)
    me_m = zh * NX + x

    def row_of(zh_, y_, x_):
        return (zh_ * NY + y_) * NX + x_

    def yrow(d):
        return row_of(zh, lax.rem(y + (NY + d), NY), x)

    def xrow(d):
        return row_of(zh, y, lax.rem(x + (NX + d), NX))

    row_z = row_of(1 - zh, y, x)
    row_f = row_of(lax.div(chan, NX), y, lax.rem(chan, NX))
    self_f = me_m == chan
    sibling = zl * NC + (1 - core)
    z_two = lax.rem(zl + 2, NZL)
    z_pair = zl + 1 - 2 * lax.rem(zl, 2)
    z_inner = NZL - 1 - zl
    inner = jnp.logical_and(zl > 0, zl < NZL - 1)

    bar = pltpu.get_barrier_semaphore()

    def greet(r, c):
        pl.semaphore_signal(bar, inc=1, device_id=(r, c), device_id_type=MESH)

    for s in range(1, NCH):
        greet(row, lax.rem(chan + s, NCH))
    for r in (yrow(2), yrow(-2), xrow(2), yrow(1), yrow(-1), xrow(1), xrow(-1)):
        greet(r, chan)
    at_z = 4 * zh + zl + jnp.where(zl < 2, 7 - zl, 12 - zl)
    greet(row_of(lax.rem(lax.div(at_z, NZL), NZH), y, x), lax.rem(at_z, NZL) * NC + core)

    sends = []

    def send(src, dst, ssem, rsem, r, c, when=None):
        copy = pltpu.make_async_remote_copy(
            src_ref=src, dst_ref=dst, send_sem=ssem, recv_sem=rsem,
            device_id=(r, c), device_id_type=MESH,
        )
        if when is None:
            copy.start()
        else:
            pl.when(when)(copy.start)
        sends.append((copy, when))

    def drain(keep):
        while len(sends) > keep:
            copy, when = sends.pop(0)
            if when is None:
                copy.wait_send()
            else:
                pl.when(when)(copy.wait_send)

    def arrived(ref, ssem, rsem):
        pltpu.make_async_remote_copy(
            src_ref=ref, dst_ref=ref, send_sem=ssem, recv_sem=rsem,
            device_id=(row, sibling), device_id_type=MESH,
        ).wait_recv()

    for load in loads:
        load.wait()

    for t in range(T):
        xf[t] = pair[:, :, t * KC:(t + 1) * KC].astype(F32).reshape(128, KC)
        for r in range(8):
            xb[t, chan, r] = xf[t, pl.ds(r, 16, stride=8), :].astype(BF16)
    lane16 = lax.broadcasted_iota(jnp.int32, (16, 128), 1)
    cols = [column(v[...].astype(F32)) for v in (ig, ib, og, ob)]
    block = jnp.zeros((16, 128), F32)
    for n, col in enumerate(cols):
        block = jnp.where(lane16 == n, jnp.broadcast_to(col, (16, 128)), block)
    pm[chan] = block

    pl.semaphore_wait(bar, jnp.where(inner, NCH - 1 + 7, NCH - 1 + 7 + 2))

    for s in range(1, NCH):
        send(pm.at[chan], pm.at[chan], ps_sem.at[s], pr_sem.at[chan], row, lax.rem(chan + s, NCH))

    def send_in(t):
        for n, (z, when) in enumerate(((z_two, None), (z_inner, inner), (z_pair, None))):
            send(xb.at[t, chan], xb.at[t, chan], xs_sem.at[t, 1 + n], xr_sem.at[t, chan], row, z * NC + core, when)
        send(xb.at[t, chan], xb.at[t, chan], xs_sem.at[t, 0], xr_sem.at[t, chan], row, sibling)

    for t in range(AHEAD):
        send_in(t)

    ki = lax.broadcasted_iota(jnp.int32, (512, 512), 0)
    ni = lax.broadcasted_iota(jnp.int32, (512, 512), 1)
    kx, ky, kp, k8 = ki >> 7, (ki >> 4) & 7, (ki >> 3) & 1, ki & 7
    want = (kp << 8) | (ky << 5) | (kx << 3) | k8
    perm[...] = jnp.where(want == ni, 1.0, 0.0).astype(BF16)
    eye_a = lax.broadcasted_iota(jnp.int32, (128, 128), 0)
    eye_b = lax.broadcasted_iota(jnp.int32, (128, 128), 1)
    eye = jnp.where(eye_a == eye_b, 1.0, 0.0).astype(BF16)
    turned = lax.dot_general(eye, wo[...], (((1,), (1,)), ((), ())), preferred_element_type=F32).astype(BF16)
    ha = lax.broadcasted_iota(jnp.int32, (128, 64), 0)
    hb = lax.broadcasted_iota(jnp.int32, (128, 64), 1)
    for par in range(2):
        pick = jnp.where(ha == 2 * hb + par, 1.0, 0.0).astype(BF16)
        wot[par * 128:(par + 1) * 128, :] = dot(turned, pick).astype(BF16)

    wt = jnp.concatenate([w[...].reshape(64, 128), gw[...]], axis=0)
    for s in range(1, NCH):
        c = lax.rem(chan + s, NCH)
        arrived(pm.at[c], ps_sem.at[s], pr_sem.at[c])
    pmv = pm[...].reshape(128, 128)
    gb[0] = jnp.broadcast_to(pmv[:, 0:1], (128, 128))
    gb[1] = jnp.broadcast_to(pmv[:, 1:2], (128, 128))
    row_valid = [tm_s[row * 8 + r].astype(F32) for r in range(8)]

    def gather_in(t):
        for n, z in enumerate((z_two, z_pair, z_inner)):
            c = z * NC + core
            arrived(xb.at[t, c], xs_sem.at[t, 0], xr_sem.at[t, c])
            if n == 0:
                send(xb.at[t, c], xb.at[t, c], xs_sem.at[t, 4], xr_sem.at[t, c], row, z_pair * NC + core, inner)
            send(xb.at[t, c], xb.at[t, c], xs_sem.at[t, 5 + n], xr_sem.at[t, c], row, sibling)
        for d in range(NZL):
            c = lax.rem(zl + d, NZL) * NC + (1 - core)
            arrived(xb.at[t, c], xs_sem.at[t, 0], xr_sem.at[t, c])

    def project(t):
        pieces = []
        gain = gb[0]
        bias = gb[1]
        for r in range(8):
            v = xb[t, :, r].astype(F32).reshape(128, KC)
            mean = jnp.sum(v, axis=0, keepdims=True) * (1.0 / 128)
            center = v - mean
            spread = jnp.sum(center * center, axis=0, keepdims=True) * (1.0 / 128)
            pieces.append((center * lax.rsqrt(spread + EPS) * gain + bias).astype(BF16))
        normed = jnp.concatenate(pieces, axis=1)
        proj = dot(wt, normed)
        col_valid = tm_v[:, t * KC:(t + 1) * KC].astype(F32)
        mask = jnp.concatenate([col_valid * s for s in row_valid], axis=1)
        left = jax.nn.sigmoid(proj[16:32]) * proj[0:16] * mask
        right = jax.nn.sigmoid(proj[48:64]) * proj[32:48] * mask
        g = jax.nn.sigmoid(proj[64:80])
        for r in range(8):
            lr_f[0, pl.ds(r, 16, stride=8), :] = left[:, r * KC:(r + 1) * KC]
            lr_f[1, pl.ds(r, 16, stride=8), :] = right[:, r * KC:(r + 1) * KC]
            gate[r, :, t * KC:(t + 1) * KC] = g[:, r * KC:(r + 1) * KC]
        lb[t, me_m] = lr_f[0].astype(BF16)
        rb[t, y] = lr_f[1].astype(BF16)

    def lslot(far, d):
        return (1 - zh if far else zh) * NX + lax.rem(x + (NX + d), NX)

    def rslot(d):
        return lax.rem(y + (NY + d), NY)

    def send_l(t, n, slot, r):
        send(lb.at[t, slot], lb.at[t, slot], ls_sem.at[t, n], lr_sem.at[t, slot], r, chan)

    def send_r(t, n, slot, r):
        send(rb.at[t, slot], rb.at[t, slot], rs_sem.at[t, n], rr_sem.at[t, slot], r, chan)

    def got_l(t, slot):
        arrived(lb.at[t, slot], ls_sem.at[t, 0], lr_sem.at[t, slot])

    def got_r(t, slot):
        arrived(rb.at[t, slot], rs_sem.at[t, 0], rr_sem.at[t, slot])

    def step1(t):
        send_l(t, 0, me_m, row_z)
        send_r(t, 0, y, yrow(2))
        send_r(t, 1, y, yrow(-2))
        send_r(t, 2, y, yrow(1))
        send_r(t, 3, y, yrow(-1))
        send_l(t, 1, me_m, xrow(2))
        send_l(t, 2, me_m, xrow(1))
        send_l(t, 3, me_m, xrow(-1))

    def step2(t):
        got_r(t, rslot(-2))
        if t % 2 == 0:
            send_r(t, 6, rslot(-2), yrow(2))
        send_r(t, 4, rslot(-2), yrow(1))
        got_r(t, rslot(2))
        if t % 2 == 1:
            send_r(t, 6, rslot(2), yrow(-2))
        send_r(t, 5, rslot(2), yrow(-1))
        got_l(t, lslot(True, 0))
        send_l(t, 4, lslot(True, 0), xrow(2))
        send_l(t, 5, lslot(True, 0), xrow(1))
        send_l(t, 6, lslot(True, 0), xrow(-1))

    def step3(t):
        for d in (-1, 1, 2):
            got_l(t, lslot(False, d))
            got_l(t, lslot(True, d))
        for d in (-1, 1, -3, 3, 4):
            got_r(t, rslot(d))
        for h in range(8):
            a = lb[t, :, 16 * h:16 * h + 16, :].reshape(128, KC)
            b = rb[t, :, 16 * h:16 * h + 16, :].reshape(128, KC)
            part = lax.dot_general(a, b, (((1,), (1,)), ((), ())), preferred_element_type=F32)
            if t == 0:
                acc[h] = part
            else:
                acc[h] += part

    for wave in range(T + 2):
        if wave < T:
            gather_in(wave)
            if wave + AHEAD < T:
                send_in(wave + AHEAD)
            project(wave)
            step1(wave)
        for back, step in ((1, step2), (2, step3)):
            if 0 <= wave - back < T:
                step(wave - back)

    lane = lax.broadcasted_iota(jnp.int32, (1, 128), 1)
    even = ((lane >> 3) & 1) == 0

    for h in range(8):
        o = acc[h].reshape(8, 2, 8, 128)
        own = jnp.where(even, o[:, 0].reshape(64, 128), o[:, 1].reshape(64, 128))
        e_f[pl.ds(h, 64, stride=8), :] = own
    es[...] = e_f[...].astype(BF16).reshape(8, 64, 128)
    for s in range(1, NCH):
        c = lax.rem(chan + s, NCH)
        send(es.at[c], er.at[chan], es_sem.at[s], er_sem.at[chan], row, c)
    er[chan] = es[chan]
    drain(NCH - 1)
    for s in range(1, NCH):
        c = lax.rem(chan + s, NCH)
        arrived(er.at[c], es_sem.at[s], er_sem.at[c])

    tri = er[...].astype(F32).reshape(8, 8, 8, 128)

    def across(v):
        return v + jnp.where(even, pltpu.roll(v, 120, 1), pltpu.roll(v, 8, 1))

    mean = across(jnp.sum(jnp.sum(tri, axis=0), axis=1)) * (1.0 / 128)
    center = tri - mean[None, :, None, :]
    spread = across(jnp.sum(jnp.sum(center * center, axis=0), axis=1)) * (1.0 / 128)
    inverse = lax.rsqrt(spread + EPS)
    e_f[0:128, :] = pmv
    g_e = e_f[pl.ds(0, 64, stride=2), :]
    g_o = e_f[pl.ds(1, 64, stride=2), :]
    gain = jnp.where(even, g_e[:, 2:3], g_o[:, 2:3])
    bias = jnp.where(even, g_e[:, 3:4], g_o[:, 3:4])
    hidden = jnp.concatenate(
        [
            (center[:, r].reshape(64, 128) * inverse[r:r + 1] * gain + bias).astype(BF16)
            for r in range(8)
        ],
        axis=1,
    )
    both = dot(wot[...], hidden)
    for q in range(4):
        a0 = both[0:128, 256 * q:256 * q + 128]
        a1 = both[0:128, 256 * q + 128:256 * q + 256]
        b0 = both[128:256, 256 * q:256 * q + 128]
        b1 = both[128:256, 256 * q + 128:256 * q + 256]
        mixed = jnp.where(even, a0 + pltpu.roll(b0, 120, 1), b1 + pltpu.roll(a1, 8, 1))
        fs[:, q] = mixed.astype(BF16).reshape(8, 16, 128)

    def f_copy():
        return pltpu.make_async_remote_copy(
            src_ref=fs.at[chan], dst_ref=fr.at[me_m], send_sem=fs_sem.at[0], recv_sem=fr_sem.at[me_m],
            device_id=(row_f, chan), device_id_type=MESH,
        )

    for s in range(1, NCH):
        c = lax.rem(chan + s, NCH)
        send(fs.at[c], fr.at[me_m], fs_sem.at[s], fr_sem.at[me_m], row_f, c)

    @pl.when(jnp.logical_not(self_f))
    def _():
        f_copy().start()

    @pl.when(self_f)
    def _():
        fr[me_m] = fs[chan]

    drain(NCH - 1)

    for s in range(1, NCH):
        m = lax.rem(me_m + s, NCH)
        arrived(fr.at[m], fs_sem.at[s], fr_sem.at[m])

    @pl.when(jnp.logical_not(self_f))
    def _():
        arrived(fr.at[me_m], fs_sem.at[0], fr_sem.at[me_m])

    for z in range(NZH):
        got = jnp.concatenate([fr[z * NX + i].reshape(64, 128) for i in range(NX)], axis=1)
        o = dot(got, perm[...])
        for q in range(4):
            for par in range(2):
                r = 2 * q + par
                val = o[16 * q:16 * q + 16, 256 * par:256 * par + 256] * gate[r, :, 256 * z:256 * z + 256]
                for half in range(2):
                    o_f[2 * z + half, pl.ds(r, 16, stride=8), :] = val[:, 128 * half:128 * half + 128]
    for n in range(4):
        out[:, :, 128 * n:128 * n + 128] = o_f[n].reshape(16, 8, 128).astype(BF16)

    drain(0)

    @pl.when(jnp.logical_not(self_f))
    def _():
        f_copy().wait_send()


def body(pair_in, token_mask, in_gain, in_bias, in_weight, out_gain, out_bias, out_weight, gate_weight):
    vm = pl.BlockSpec(memory_space=pltpu.VMEM)
    sm = pl.BlockSpec(memory_space=pltpu.SMEM)
    dma = pltpu.SemaphoreType.DMA
    return pl.pallas_call(
        kernel,
        out_shape=jax.ShapeDtypeStruct((16, 8, 512), BF16),
        in_specs=[sm] + [pl.BlockSpec(memory_space=pltpu.HBM)] * 9,
        out_specs=vm,
        scratch_shapes=[
            pltpu.VMEM((16, 8, 512), BF16),
            pltpu.VMEM((1, 512), jnp.int32),
            pltpu.VMEM((1, 16), BF16),
            pltpu.VMEM((1, 16), BF16),
            pltpu.VMEM((4, 16, 128), BF16),
            pltpu.VMEM((1, 16), F32),
            pltpu.VMEM((1, 16), F32),
            pltpu.VMEM((128, 128), BF16),
            pltpu.VMEM((16, 128), BF16),
            dma((9,)),
            pltpu.VMEM((T, 128, KC), F32),
            pltpu.VMEM((T, NCH, 8, 16, KC), BF16),
            pltpu.VMEM((NCH, 16, 128), F32),
            pltpu.VMEM((2, 128, 128), F32),
            pltpu.VMEM((2, 128, KC), F32),
            pltpu.VMEM((T, 8, 128, KC), BF16),
            pltpu.VMEM((T, 8, 128, KC), BF16),
            pltpu.VMEM((8, 128, 128), F32),
            pltpu.VMEM((512, 128), F32),
            pltpu.VMEM((8, 64, 128), BF16),
            pltpu.VMEM((8, 64, 128), BF16),
            pltpu.VMEM((8, 4, 16, 128), BF16),
            pltpu.VMEM((8, 4, 16, 128), BF16),
            pltpu.VMEM((8, 16, 512), F32),
            pltpu.VMEM((512, 512), BF16),
            pltpu.VMEM((256, 64), BF16),
            pltpu.VMEM((4, 128, 128), F32),
            dma((T, 8)), dma((T, NCH)),
            dma((NCH,)), dma((NCH,)),
            dma((T, 7)), dma((T, 8)),
            dma((T, 7)), dma((T, 8)),
            dma((NCH,)), dma((NCH,)),
            dma((NCH,)), dma((NCH,)),
        ],
        compiler_params=pltpu.CompilerParams(
            collective_id=0, has_side_effects=True, vmem_limit_bytes=60 * 1024 * 1024
        ),
    )(
        token_mask,
        pair_in,
        token_mask.reshape(1, 512),
        in_gain.reshape(1, 16),
        in_bias.reshape(1, 16),
        jnp.transpose(in_weight, (0, 2, 1)),
        out_gain.reshape(1, 16),
        out_bias.reshape(1, 16),
        out_weight,
        gate_weight.T,
    )


def solution(mesh):
    return jax.shard_map(
        body,
        mesh=mesh,
        in_specs=(
            P("chan", "row", None),
            P(),
            P("chan"),
            P("chan"),
            P(None, None, "chan"),
            P("chan"),
            P("chan"),
            P(),
            P(None, "chan"),
        ),
        out_specs=P("chan", "row", None),
        check_vma=False,
    )
```

```python
import jax
import jax.numpy as jnp
from jax import lax
from jax.experimental import pallas as pl
from jax.experimental.pallas import tpu as pltpu
from jax.sharding import PartitionSpec as P

MESH = pl.DeviceIdType.MESH
EPS = 1e-05
NZH, NY, NX, NZL, NC = 2, 8, 4, 4, 2
NCH = NZL * NC
T = 4
KC = 128
AHEAD = 2
ORDER = (
    ("relay", 0), ("send", 2), ("relay", 1), ("in", 0), ("send", 3), ("proj", 0), ("s1", 0), ("relay", 2),
    ("in", 1), ("proj", 1), ("s1", 1), ("relay", 3), ("s2", 0),
    ("in", 2), ("proj", 2), ("s1", 2), ("s2l", 0), ("s2", 1),
    ("in", 3), ("proj", 3), ("s1", 3), ("s2l", 1), ("s2", 2), ("s2l", 2), ("s2", 3), ("s3", 0), ("s3", 1),
    ("s2l", 3), ("s3", 2), ("s3", 3),
)
F32 = jnp.float32
BF16 = jnp.bfloat16


def dot(a, b):
    return jnp.dot(a, b, preferred_element_type=F32)


def column(vec):
    n = vec.shape[1]
    a = lax.broadcasted_iota(jnp.int32, (n, n), 0)
    b = lax.broadcasted_iota(jnp.int32, (n, n), 1)
    return jnp.sum(jnp.where(a == b, jnp.broadcast_to(vec, (n, n)), 0.0), axis=1, keepdims=True)


def kernel(
    *refs,
):
    ins, (out, *vins), (sem_in, *rest) = refs[:10], refs[10:21], refs[21:]
    run(ins, out, vins, sem_in, *rest)


def run(
    ins, out, vins, sem_in,
    xf, xb, pm, gb, lr_f, lb, rb, acc, e_f, es, er, fs, fr, gate, perm, wot, o_f,
    xs_sem, xr_sem, ps_sem, pr_sem, ls_sem, lr_sem, rs_sem, rr_sem, es_sem, er_sem, fs_sem, fr_sem,
):
    loads = [pltpu.make_async_copy(a, b, sem_in.at[n]) for n, (a, b) in enumerate(zip(ins, vins))]
    for load in loads:
        load.start()
    pair, ig, ib, og, ob, tm_v, w, wo, gw, tm_s = vins
    row = lax.axis_index("row")
    chan = lax.axis_index("chan")
    zh = lax.div(row, NY * NX)
    y = lax.rem(lax.div(row, NX), NY)
    x = lax.rem(row, NX)
    zl = lax.div(chan, NC)
    core = lax.rem(chan, NC)
    me_m = zh * NX + x

    def row_of(zh_, y_, x_):
        return (zh_ * NY + y_) * NX + x_

    def yrow(d):
        return row_of(zh, lax.rem(y + (NY + d), NY), x)

    def xrow(d):
        return row_of(zh, y, lax.rem(x + (NX + d), NX))

    row_z = row_of(1 - zh, y, x)
    row_f = row_of(lax.div(chan, NX), y, lax.rem(chan, NX))
    self_f = me_m == chan
    sibling = zl * NC + (1 - core)
    z_two = lax.rem(zl + 2, NZL)
    z_pair = zl + 1 - 2 * lax.rem(zl, 2)
    z_inner = NZL - 1 - zl
    inner = jnp.logical_and(zl > 0, zl < NZL - 1)

    bar = pltpu.get_barrier_semaphore()

    def greet(r, c):
        pl.semaphore_signal(bar, inc=1, device_id=(r, c), device_id_type=MESH)

    for s in range(1, NCH):
        greet(row, lax.rem(chan + s, NCH))
    for r in (yrow(2), yrow(-2), xrow(2), yrow(1), yrow(-1), xrow(1), xrow(-1)):
        greet(r, chan)
    at_z = 4 * zh + zl + jnp.where(zl < 2, 7 - zl, 12 - zl)
    greet(row_of(lax.rem(lax.div(at_z, NZL), NZH), y, x), lax.rem(at_z, NZL) * NC + core)

    sends = []

    def send(src, dst, ssem, rsem, r, c, when=None):
        copy = pltpu.make_async_remote_copy(
            src_ref=src, dst_ref=dst, send_sem=ssem, recv_sem=rsem,
            device_id=(r, c), device_id_type=MESH,
        )
        if when is None:
            copy.start()
        else:
            pl.when(when)(copy.start)
        sends.append((copy, when))

    def drain(keep):
        while len(sends) > keep:
            copy, when = sends.pop(0)
            if when is None:
                copy.wait_send()
            else:
                pl.when(when)(copy.wait_send)

    def arrived(ref, ssem, rsem):
        pltpu.make_async_remote_copy(
            src_ref=ref, dst_ref=ref, send_sem=ssem, recv_sem=rsem,
            device_id=(row, sibling), device_id_type=MESH,
        ).wait_recv()

    for load in loads[:5]:
        load.wait()

    for t in range(T):
        xf[t] = pair[:, :, t * KC:(t + 1) * KC].astype(F32).reshape(128, KC)
        for r in range(8):
            xb[t, chan, r] = xf[t, pl.ds(r, 16, stride=8), :].astype(BF16)
    lane16 = lax.broadcasted_iota(jnp.int32, (16, 128), 1)
    cols = [column(v[...].astype(F32)) for v in (ig, ib, og, ob)]
    block = jnp.zeros((16, 128), F32)
    for n, col in enumerate(cols):
        block = jnp.where(lane16 == n, jnp.broadcast_to(col, (16, 128)), block)
    pm[chan] = block

    pl.semaphore_wait(bar, jnp.where(inner, NCH - 1 + 7, NCH - 1 + 7 + 2))

    for s in range(1, NCH):
        send(pm.at[chan], pm.at[chan], ps_sem.at[s], pr_sem.at[chan], row, lax.rem(chan + s, NCH))

    def send_in(t):
        for n, (z, when) in enumerate(((z_two, None), (z_inner, inner), (z_pair, None))):
            send(xb.at[t, chan], xb.at[t, chan], xs_sem.at[t, 1 + n], xr_sem.at[t, chan], row, z * NC + core, when)
        send(xb.at[t, chan], xb.at[t, chan], xs_sem.at[t, 0], xr_sem.at[t, chan], row, sibling)

    for t in range(AHEAD):
        send_in(t)

    for load in loads[5:]:
        load.wait()

    ki = lax.broadcasted_iota(jnp.int32, (512, 512), 0)
    ni = lax.broadcasted_iota(jnp.int32, (512, 512), 1)
    kx, ky, kp, k8 = ki >> 7, (ki >> 4) & 7, (ki >> 3) & 1, ki & 7
    want = (kp << 8) | (ky << 5) | (kx << 3) | k8
    perm[...] = jnp.where(want == ni, 1.0, 0.0).astype(BF16)
    eye_a = lax.broadcasted_iota(jnp.int32, (128, 128), 0)
    eye_b = lax.broadcasted_iota(jnp.int32, (128, 128), 1)
    eye = jnp.where(eye_a == eye_b, 1.0, 0.0).astype(BF16)
    turned = lax.dot_general(eye, wo[...], (((1,), (1,)), ((), ())), preferred_element_type=F32).astype(BF16)
    ha = lax.broadcasted_iota(jnp.int32, (128, 64), 0)
    hb = lax.broadcasted_iota(jnp.int32, (128, 64), 1)
    for par in range(2):
        pick = jnp.where(ha == 2 * hb + par, 1.0, 0.0).astype(BF16)
        wot[par * 128:(par + 1) * 128, :] = dot(turned, pick).astype(BF16)

    wt = jnp.concatenate([w[...].reshape(64, 128), gw[...]], axis=0)
    for s in range(1, NCH):
        c = lax.rem(chan + s, NCH)
        arrived(pm.at[c], ps_sem.at[s], pr_sem.at[c])
    pmv = pm[...].reshape(128, 128)
    gb[0] = jnp.broadcast_to(pmv[:, 0:1], (128, 128))
    gb[1] = jnp.broadcast_to(pmv[:, 1:2], (128, 128))
    row_valid = [tm_s[row * 8 + r].astype(F32) for r in range(8)]

    early = []

    def relay(t):
        c = z_two * NC + core
        arrived(xb.at[t, c], xs_sem.at[t, 0], xr_sem.at[t, c])
        send(xb.at[t, c], xb.at[t, c], xs_sem.at[t, 4], xr_sem.at[t, c], row, z_pair * NC + core, inner)
        early.append(t)

    def gather_in(t):
        for n, z in enumerate((z_two, z_pair, z_inner)):
            c = z * NC + core
            if t not in early or n != 0:
                arrived(xb.at[t, c], xs_sem.at[t, 0], xr_sem.at[t, c])
            if n == 0 and t not in early:
                send(xb.at[t, c], xb.at[t, c], xs_sem.at[t, 4], xr_sem.at[t, c], row, z_pair * NC + core, inner)
            send(xb.at[t, c], xb.at[t, c], xs_sem.at[t, 5 + n], xr_sem.at[t, c], row, sibling)
        for d in range(NZL):
            c = lax.rem(zl + d, NZL) * NC + (1 - core)
            arrived(xb.at[t, c], xs_sem.at[t, 0], xr_sem.at[t, c])

    def project(t):
        pieces = []
        gain = gb[0]
        bias = gb[1]
        for r in range(8):
            v = xb[t, :, r].astype(F32).reshape(128, KC)
            mean = jnp.sum(v, axis=0, keepdims=True) * (1.0 / 128)
            center = v - mean
            spread = jnp.sum(center * center, axis=0, keepdims=True) * (1.0 / 128)
            pieces.append((center * lax.rsqrt(spread + EPS) * gain + bias).astype(BF16))
        normed = jnp.concatenate(pieces, axis=1)
        proj = dot(wt, normed)
        col_valid = tm_v[:, t * KC:(t + 1) * KC].astype(F32)
        mask = jnp.concatenate([col_valid * s for s in row_valid], axis=1)
        left = jax.nn.sigmoid(proj[16:32]) * proj[0:16] * mask
        right = jax.nn.sigmoid(proj[48:64]) * proj[32:48] * mask
        g = jax.nn.sigmoid(proj[64:80])
        for r in range(8):
            lr_f[0, pl.ds(r, 16, stride=8), :] = left[:, r * KC:(r + 1) * KC]
            lr_f[1, pl.ds(r, 16, stride=8), :] = right[:, r * KC:(r + 1) * KC]
            gate[r, :, t * KC:(t + 1) * KC] = g[:, r * KC:(r + 1) * KC]
        lb[t, me_m] = lr_f[0].astype(BF16)
        rb[t, y] = lr_f[1].astype(BF16)

    def lslot(far, d):
        return (1 - zh if far else zh) * NX + lax.rem(x + (NX + d), NX)

    def rslot(d):
        return lax.rem(y + (NY + d), NY)

    def send_l(t, n, slot, r):
        send(lb.at[t, slot], lb.at[t, slot], ls_sem.at[t, n], lr_sem.at[t, slot], r, chan)

    def send_r(t, n, slot, r):
        send(rb.at[t, slot], rb.at[t, slot], rs_sem.at[t, n], rr_sem.at[t, slot], r, chan)

    def got_l(t, slot):
        arrived(lb.at[t, slot], ls_sem.at[t, 0], lr_sem.at[t, slot])

    def got_r(t, slot):
        arrived(rb.at[t, slot], rs_sem.at[t, 0], rr_sem.at[t, slot])

    def step1(t):
        send_l(t, 0, me_m, row_z)
        send_r(t, 0, y, yrow(2))
        send_r(t, 1, y, yrow(-2))
        send_r(t, 2, y, yrow(1))
        send_r(t, 3, y, yrow(-1))
        send_l(t, 1, me_m, xrow(2))
        send_l(t, 2, me_m, xrow(1))
        send_l(t, 3, me_m, xrow(-1))

    def step2(t):
        got_r(t, rslot(-2))
        if t % 2 == 0:
            send_r(t, 6, rslot(-2), yrow(2))
        send_r(t, 4, rslot(-2), yrow(1))
        got_r(t, rslot(2))
        if t % 2 == 1:
            send_r(t, 6, rslot(2), yrow(-2))
        send_r(t, 5, rslot(2), yrow(-1))

    def step2l(t):
        got_l(t, lslot(True, 0))
        send_l(t, 4, lslot(True, 0), xrow(2))
        send_l(t, 5, lslot(True, 0), xrow(1))
        send_l(t, 6, lslot(True, 0), xrow(-1))

    def step3(t):
        for d in (-1, 1, 2):
            got_l(t, lslot(False, d))
            got_l(t, lslot(True, d))
        for d in (-1, 1, -3, 3, 4):
            got_r(t, rslot(d))
        for h in range(8):
            a = lb[t, :, 16 * h:16 * h + 16, :].reshape(128, KC)
            b = rb[t, :, 16 * h:16 * h + 16, :].reshape(128, KC)
            part = lax.dot_general(a, b, (((1,), (1,)), ((), ())), preferred_element_type=F32)
            if t == 0:
                acc[h] = part
            else:
                acc[h] += part

    for step, t in ORDER:
        {"in": gather_in, "send": send_in, "relay": relay, "proj": project, "s1": step1, "s2": step2, "s2l": step2l, "s3": step3}[step](t)

    lane = lax.broadcasted_iota(jnp.int32, (1, 128), 1)
    even = ((lane >> 3) & 1) == 0

    for h in range(8):
        o = acc[h].reshape(8, 2, 8, 128)
        own = jnp.where(even, o[:, 0].reshape(64, 128), o[:, 1].reshape(64, 128))
        e_f[pl.ds(h, 64, stride=8), :] = own
    es[...] = e_f[...].astype(BF16).reshape(8, 64, 128)
    for s in range(1, NCH):
        c = lax.rem(chan + s, NCH)
        send(es.at[c], er.at[chan], es_sem.at[s], er_sem.at[chan], row, c)
    er[chan] = es[chan]
    drain(NCH - 1)
    for s in range(1, NCH):
        c = lax.rem(chan + s, NCH)
        arrived(er.at[c], es_sem.at[s], er_sem.at[c])

    tri = er[...].astype(F32).reshape(8, 8, 8, 128)

    def across(v):
        return v + jnp.where(even, pltpu.roll(v, 120, 1), pltpu.roll(v, 8, 1))

    mean = across(jnp.sum(jnp.sum(tri, axis=0), axis=1)) * (1.0 / 128)
    center = tri - mean[None, :, None, :]
    spread = across(jnp.sum(jnp.sum(center * center, axis=0), axis=1)) * (1.0 / 128)
    inverse = lax.rsqrt(spread + EPS)
    e_f[0:128, :] = pmv
    g_e = e_f[pl.ds(0, 64, stride=2), :]
    g_o = e_f[pl.ds(1, 64, stride=2), :]
    gain = jnp.where(even, g_e[:, 2:3], g_o[:, 2:3])
    bias = jnp.where(even, g_e[:, 3:4], g_o[:, 3:4])
    hidden = jnp.concatenate(
        [
            (center[:, r].reshape(64, 128) * inverse[r:r + 1] * gain + bias).astype(BF16)
            for r in range(8)
        ],
        axis=1,
    )
    both = dot(wot[...], hidden)
    for q in range(4):
        a0 = both[0:128, 256 * q:256 * q + 128]
        a1 = both[0:128, 256 * q + 128:256 * q + 256]
        b0 = both[128:256, 256 * q:256 * q + 128]
        b1 = both[128:256, 256 * q + 128:256 * q + 256]
        mixed = jnp.where(even, a0 + pltpu.roll(b0, 120, 1), b1 + pltpu.roll(a1, 8, 1))
        fs[:, q] = mixed.astype(BF16).reshape(8, 16, 128)

    def f_copy():
        return pltpu.make_async_remote_copy(
            src_ref=fs.at[chan], dst_ref=fr.at[me_m], send_sem=fs_sem.at[0], recv_sem=fr_sem.at[me_m],
            device_id=(row_f, chan), device_id_type=MESH,
        )

    for s in range(1, NCH):
        c = lax.rem(chan + s, NCH)
        send(fs.at[c], fr.at[me_m], fs_sem.at[s], fr_sem.at[me_m], row_f, c)

    @pl.when(jnp.logical_not(self_f))
    def _():
        f_copy().start()

    @pl.when(self_f)
    def _():
        fr[me_m] = fs[chan]

    drain(NCH - 1)

    for s in range(1, NCH):
        m = lax.rem(me_m + s, NCH)
        arrived(fr.at[m], fs_sem.at[s], fr_sem.at[m])

    @pl.when(jnp.logical_not(self_f))
    def _():
        arrived(fr.at[me_m], fs_sem.at[0], fr_sem.at[me_m])

    for z in range(NZH):
        got = jnp.concatenate([fr[z * NX + i].reshape(64, 128) for i in range(NX)], axis=1)
        o = dot(got, perm[...])
        for q in range(4):
            for par in range(2):
                r = 2 * q + par
                val = o[16 * q:16 * q + 16, 256 * par:256 * par + 256] * gate[r, :, 256 * z:256 * z + 256]
                for half in range(2):
                    o_f[2 * z + half, pl.ds(r, 16, stride=8), :] = val[:, 128 * half:128 * half + 128]
    for n in range(4):
        out[:, :, 128 * n:128 * n + 128] = o_f[n].reshape(16, 8, 128).astype(BF16)

    drain(0)

    @pl.when(jnp.logical_not(self_f))
    def _():
        f_copy().wait_send()


def body(pair_in, token_mask, in_gain, in_bias, in_weight, out_gain, out_bias, out_weight, gate_weight):
    vm = pl.BlockSpec(memory_space=pltpu.VMEM)
    dma = pltpu.SemaphoreType.DMA
    return pl.pallas_call(
        kernel,
        out_shape=pltpu.VMEM((16, 8, 512), BF16),
        in_specs=[pl.BlockSpec(memory_space=pltpu.HBM)] * 10,
        out_specs=vm,
        scratch_shapes=[
            pltpu.VMEM((16, 8, 512), BF16),
            pltpu.VMEM((1, 16), BF16),
            pltpu.VMEM((1, 16), BF16),
            pltpu.VMEM((1, 16), F32),
            pltpu.VMEM((1, 16), F32),
            pltpu.VMEM((1, 512), jnp.int32),
            pltpu.VMEM((4, 16, 128), BF16),
            pltpu.VMEM((128, 128), BF16),
            pltpu.VMEM((16, 128), BF16),
            pltpu.SMEM((512,), jnp.int32),
            dma((10,)),
            pltpu.VMEM((T, 128, KC), F32),
            pltpu.VMEM((T, NCH, 8, 16, KC), BF16),
            pltpu.VMEM((NCH, 16, 128), F32),
            pltpu.VMEM((2, 128, 128), F32),
            pltpu.VMEM((2, 128, KC), F32),
            pltpu.VMEM((T, 8, 128, KC), BF16),
            pltpu.VMEM((T, 8, 128, KC), BF16),
            pltpu.VMEM((8, 128, 128), F32),
            pltpu.VMEM((512, 128), F32),
            pltpu.VMEM((8, 64, 128), BF16),
            pltpu.VMEM((8, 64, 128), BF16),
            pltpu.VMEM((8, 4, 16, 128), BF16),
            pltpu.VMEM((8, 4, 16, 128), BF16),
            pltpu.VMEM((8, 16, 512), F32),
            pltpu.VMEM((512, 512), BF16),
            pltpu.VMEM((256, 64), BF16),
            pltpu.VMEM((4, 128, 128), F32),
            dma((T, 8)), dma((T, NCH)),
            dma((NCH,)), dma((NCH,)),
            dma((T, 7)), dma((T, 8)),
            dma((T, 7)), dma((T, 8)),
            dma((NCH,)), dma((NCH,)),
            dma((NCH,)), dma((NCH,)),
        ],
        compiler_params=pltpu.CompilerParams(
            collective_id=0, has_side_effects=True, vmem_limit_bytes=60 * 1024 * 1024
        ),
    )(
        pair_in,
        in_gain.reshape(1, 16),
        in_bias.reshape(1, 16),
        out_gain.reshape(1, 16),
        out_bias.reshape(1, 16),
        token_mask.reshape(1, 512),
        jnp.transpose(in_weight, (0, 2, 1)),
        out_weight,
        gate_weight.T,
        token_mask,
    )


def solution(mesh):
    return jax.shard_map(
        body,
        mesh=mesh,
        in_specs=(
            P("chan", "row", None),
            P(),
            P("chan"),
            P("chan"),
            P(None, None, "chan"),
            P("chan"),
            P("chan"),
            P(),
            P(None, "chan"),
        ),
        out_specs=P("chan", "row", None),
        check_vma=False,
    )
```

```python
import jax
import jax.numpy as jnp
from jax import lax
from jax.experimental import pallas as pl
from jax.experimental.pallas import tpu as pltpu
from jax.sharding import PartitionSpec as P

MESH = pl.DeviceIdType.MESH
EPS = 1e-05
NZH, NY, NX, NZL, NC = 2, 8, 4, 4, 2
NCH = NZL * NC
T = 4
KC = 128
AHEAD = 2
ORDER = (
    ("relay", 0), ("send", 2), ("relay", 1), ("par", 0), ("in", 0), ("send", 3), ("proj", 0), ("s1", 0), ("relay", 2),
    ("in", 1), ("proj", 1), ("s1", 1), ("relay", 3), ("s2", 0),
    ("in", 2), ("proj", 2), ("s1", 2), ("s2l", 0), ("s2", 1),
    ("in", 3), ("proj", 3), ("s1", 3), ("s2l", 1), ("s2", 2), ("s2l", 2), ("s2", 3), ("s3", 0), ("s3", 1),
    ("s2l", 3), ("s3", 2), ("s3", 3),
)
F32 = jnp.float32
BF16 = jnp.bfloat16


def dot(a, b):
    return jnp.dot(a, b, preferred_element_type=F32)


def column(vec):
    n = vec.shape[1]
    a = lax.broadcasted_iota(jnp.int32, (n, n), 0)
    b = lax.broadcasted_iota(jnp.int32, (n, n), 1)
    return jnp.sum(jnp.where(a == b, jnp.broadcast_to(vec, (n, n)), 0.0), axis=1, keepdims=True)


def kernel(
    *refs,
):
    ins, (out, *vins), (sem_in, *rest) = refs[:10], refs[10:21], refs[21:]
    run(ins, out, vins, sem_in, *rest)


def run(
    ins, out, vins, sem_in,
    xf, xb, pm, gb, lr_f, lb, rb, acc, e_f, es, er, fs, fr, gate, perm, wot, o_f,
    xs_sem, xr_sem, ps_sem, pr_sem, ls_sem, lr_sem, rs_sem, rr_sem, es_sem, er_sem, fs_sem, fr_sem,
):
    loads = [pltpu.make_async_copy(a, b, sem_in.at[n]) for n, (a, b) in enumerate(zip(ins, vins))]
    for load in loads:
        load.start()
    pair, ig, ib, og, ob, tm_v, w, wo, gw, tm_s = vins
    row = lax.axis_index("row")
    chan = lax.axis_index("chan")
    zh = lax.div(row, NY * NX)
    y = lax.rem(lax.div(row, NX), NY)
    x = lax.rem(row, NX)
    zl = lax.div(chan, NC)
    core = lax.rem(chan, NC)
    me_m = zh * NX + x

    def row_of(zh_, y_, x_):
        return (zh_ * NY + y_) * NX + x_

    def yrow(d):
        return row_of(zh, lax.rem(y + (NY + d), NY), x)

    def xrow(d):
        return row_of(zh, y, lax.rem(x + (NX + d), NX))

    row_z = row_of(1 - zh, y, x)
    row_f = row_of(lax.div(chan, NX), y, lax.rem(chan, NX))
    self_f = me_m == chan
    sibling = zl * NC + (1 - core)
    z_two = lax.rem(zl + 2, NZL)
    z_pair = zl + 1 - 2 * lax.rem(zl, 2)
    z_inner = NZL - 1 - zl
    inner = jnp.logical_and(zl > 0, zl < NZL - 1)

    bar = pltpu.get_barrier_semaphore()

    def greet(r, c):
        pl.semaphore_signal(bar, inc=1, device_id=(r, c), device_id_type=MESH)

    for s in range(1, NCH):
        greet(row, lax.rem(chan + s, NCH))
    for r in (yrow(2), yrow(-2), xrow(2), yrow(1), yrow(-1), xrow(1), xrow(-1)):
        greet(r, chan)
    at_z = 4 * zh + zl + jnp.where(zl < 2, 7 - zl, 12 - zl)
    greet(row_of(lax.rem(lax.div(at_z, NZL), NZH), y, x), lax.rem(at_z, NZL) * NC + core)

    sends = []

    def send(src, dst, ssem, rsem, r, c, when=None):
        copy = pltpu.make_async_remote_copy(
            src_ref=src, dst_ref=dst, send_sem=ssem, recv_sem=rsem,
            device_id=(r, c), device_id_type=MESH,
        )
        if when is None:
            copy.start()
        else:
            pl.when(when)(copy.start)
        sends.append((copy, when))

    def drain(keep):
        while len(sends) > keep:
            copy, when = sends.pop(0)
            if when is None:
                copy.wait_send()
            else:
                pl.when(when)(copy.wait_send)

    def arrived(ref, ssem, rsem):
        pltpu.make_async_remote_copy(
            src_ref=ref, dst_ref=ref, send_sem=ssem, recv_sem=rsem,
            device_id=(row, sibling), device_id_type=MESH,
        ).wait_recv()

    def prepare(t):
        xf[t] = pair[:, :, t * KC:(t + 1) * KC].astype(F32).reshape(128, KC)
        for r in range(8):
            xb[t, chan, r] = xf[t, pl.ds(r, 16, stride=8), :].astype(BF16)

    def send_in(t):
        for n, (z, when) in enumerate(((z_two, None), (z_inner, inner), (z_pair, None))):
            send(xb.at[t, chan], xb.at[t, chan], xs_sem.at[t, 1 + n], xr_sem.at[t, chan], row, z * NC + core, when)
        send(xb.at[t, chan], xb.at[t, chan], xs_sem.at[t, 0], xr_sem.at[t, chan], row, sibling)

    for load in loads[1:5]:
        load.wait()
    lane16 = lax.broadcasted_iota(jnp.int32, (16, 128), 1)
    cols = [column(v[...].astype(F32)) for v in (ig, ib, og, ob)]
    block = jnp.zeros((16, 128), F32)
    for n, col in enumerate(cols):
        block = jnp.where(lane16 == n, jnp.broadcast_to(col, (16, 128)), block)
    pm[chan] = block
    loads[0].wait()
    prepare(0)
    pl.semaphore_wait(bar, jnp.where(inner, NCH - 1 + 7, NCH - 1 + 7 + 2))
    for s in range(1, NCH):
        send(pm.at[chan], pm.at[chan], ps_sem.at[s], pr_sem.at[chan], row, lax.rem(chan + s, NCH))
    send_in(0)
    for t in range(1, AHEAD):
        prepare(t)
        send_in(t)

    for t in range(AHEAD, T):
        prepare(t)

    for load in loads[5:]:
        load.wait()

    ki = lax.broadcasted_iota(jnp.int32, (512, 512), 0)
    ni = lax.broadcasted_iota(jnp.int32, (512, 512), 1)
    kx, ky, kp, k8 = ki >> 7, (ki >> 4) & 7, (ki >> 3) & 1, ki & 7
    want = (kp << 8) | (ky << 5) | (kx << 3) | k8
    perm[...] = jnp.where(want == ni, 1.0, 0.0).astype(BF16)
    eye_a = lax.broadcasted_iota(jnp.int32, (128, 128), 0)
    eye_b = lax.broadcasted_iota(jnp.int32, (128, 128), 1)
    eye = jnp.where(eye_a == eye_b, 1.0, 0.0).astype(BF16)
    turned = lax.dot_general(eye, wo[...], (((1,), (1,)), ((), ())), preferred_element_type=F32).astype(BF16)
    ha = lax.broadcasted_iota(jnp.int32, (128, 64), 0)
    hb = lax.broadcasted_iota(jnp.int32, (128, 64), 1)
    for par in range(2):
        pick = jnp.where(ha == 2 * hb + par, 1.0, 0.0).astype(BF16)
        wot[par * 128:(par + 1) * 128, :] = dot(turned, pick).astype(BF16)

    wt = jnp.concatenate([w[...].reshape(64, 128), gw[...]], axis=0)

    def params(t):
        for s in range(1, NCH):
            c = lax.rem(chan + s, NCH)
            arrived(pm.at[c], ps_sem.at[s], pr_sem.at[c])
        for n in range(2):
            gb[n] = jnp.broadcast_to(pm[...].reshape(128, 128)[:, n:n + 1], (128, 128))

    row_valid = [tm_s[row * 8 + r].astype(F32) for r in range(8)]

    early = []

    def relay(t):
        c = z_two * NC + core
        arrived(xb.at[t, c], xs_sem.at[t, 0], xr_sem.at[t, c])
        send(xb.at[t, c], xb.at[t, c], xs_sem.at[t, 4], xr_sem.at[t, c], row, z_pair * NC + core, inner)
        early.append(t)

    def gather_in(t):
        for n, z in enumerate((z_two, z_pair, z_inner)):
            c = z * NC + core
            if t not in early or n != 0:
                arrived(xb.at[t, c], xs_sem.at[t, 0], xr_sem.at[t, c])
            if n == 0 and t not in early:
                send(xb.at[t, c], xb.at[t, c], xs_sem.at[t, 4], xr_sem.at[t, c], row, z_pair * NC + core, inner)
            send(xb.at[t, c], xb.at[t, c], xs_sem.at[t, 5 + n], xr_sem.at[t, c], row, sibling)
        for d in range(NZL):
            c = lax.rem(zl + d, NZL) * NC + (1 - core)
            arrived(xb.at[t, c], xs_sem.at[t, 0], xr_sem.at[t, c])

    def project(t):
        pieces = []
        gain = gb[0]
        bias = gb[1]
        for r in range(8):
            v = xb[t, :, r].astype(F32).reshape(128, KC)
            mean = jnp.sum(v, axis=0, keepdims=True) * (1.0 / 128)
            center = v - mean
            spread = jnp.sum(center * center, axis=0, keepdims=True) * (1.0 / 128)
            pieces.append((center * lax.rsqrt(spread + EPS) * gain + bias).astype(BF16))
        normed = jnp.concatenate(pieces, axis=1)
        proj = dot(wt, normed)
        col_valid = tm_v[:, t * KC:(t + 1) * KC].astype(F32)
        mask = jnp.concatenate([col_valid * s for s in row_valid], axis=1)
        left = jax.nn.sigmoid(proj[16:32]) * proj[0:16] * mask
        right = jax.nn.sigmoid(proj[48:64]) * proj[32:48] * mask
        g = jax.nn.sigmoid(proj[64:80])
        for r in range(8):
            lr_f[0, pl.ds(r, 16, stride=8), :] = left[:, r * KC:(r + 1) * KC]
            lr_f[1, pl.ds(r, 16, stride=8), :] = right[:, r * KC:(r + 1) * KC]
            gate[t, r] = g[:, r * KC:(r + 1) * KC]
        lb[t, me_m] = lr_f[0].astype(BF16)
        rb[t, y] = lr_f[1].astype(BF16)

    def lslot(far, d):
        return (1 - zh if far else zh) * NX + lax.rem(x + (NX + d), NX)

    def rslot(d):
        return lax.rem(y + (NY + d), NY)

    def send_l(t, n, slot, r):
        send(lb.at[t, slot], lb.at[t, slot], ls_sem.at[t, n], lr_sem.at[t, slot], r, chan)

    def send_r(t, n, slot, r):
        send(rb.at[t, slot], rb.at[t, slot], rs_sem.at[t, n], rr_sem.at[t, slot], r, chan)

    def got_l(t, slot):
        arrived(lb.at[t, slot], ls_sem.at[t, 0], lr_sem.at[t, slot])

    def got_r(t, slot):
        arrived(rb.at[t, slot], rs_sem.at[t, 0], rr_sem.at[t, slot])

    def step1(t):
        send_l(t, 0, me_m, row_z)
        send_r(t, 0, y, yrow(2))
        send_r(t, 1, y, yrow(-2))
        send_r(t, 2, y, yrow(1))
        send_r(t, 3, y, yrow(-1))
        send_l(t, 1, me_m, xrow(2))
        send_l(t, 2, me_m, xrow(1))
        send_l(t, 3, me_m, xrow(-1))

    def step2(t):
        got_r(t, rslot(-2))
        if t % 2 == 0:
            send_r(t, 6, rslot(-2), yrow(2))
        send_r(t, 4, rslot(-2), yrow(1))
        got_r(t, rslot(2))
        if t % 2 == 1:
            send_r(t, 6, rslot(2), yrow(-2))
        send_r(t, 5, rslot(2), yrow(-1))

    def step2l(t):
        got_l(t, lslot(True, 0))
        send_l(t, 4, lslot(True, 0), xrow(2))
        send_l(t, 5, lslot(True, 0), xrow(1))
        send_l(t, 6, lslot(True, 0), xrow(-1))

    def step3(t):
        for d in (-1, 1, 2):
            got_l(t, lslot(False, d))
            got_l(t, lslot(True, d))
        for d in (-1, 1, -3, 3, 4):
            got_r(t, rslot(d))
        for h in range(8):
            a = lb[t, :, 16 * h:16 * h + 16, :].reshape(128, KC)
            b = rb[t, :, 16 * h:16 * h + 16, :].reshape(128, KC)
            part = lax.dot_general(a, b, (((1,), (1,)), ((), ())), preferred_element_type=F32)
            if t == 0:
                acc[h] = part
            else:
                acc[h] += part

    for step, t in ORDER:
        {"in": gather_in, "send": send_in, "relay": relay, "par": params, "proj": project, "s1": step1, "s2": step2, "s2l": step2l, "s3": step3}[step](t)

    lane = lax.broadcasted_iota(jnp.int32, (1, 128), 1)
    even = ((lane >> 3) & 1) == 0

    for h in range(8):
        o = acc[h].reshape(8, 2, 8, 128)
        own = jnp.where(even, o[:, 0].reshape(64, 128), o[:, 1].reshape(64, 128))
        e_f[pl.ds(h, 64, stride=8), :] = own
    es[...] = e_f[...].astype(BF16).reshape(8, 64, 128)
    for s in range(1, NCH):
        c = lax.rem(chan + s, NCH)
        send(es.at[c], er.at[chan], es_sem.at[s], er_sem.at[chan], row, c)
    er[chan] = es[chan]
    drain(NCH - 1)
    for s in range(1, NCH):
        c = lax.rem(chan + s, NCH)
        arrived(er.at[c], es_sem.at[s], er_sem.at[c])

    tri = er[...].astype(F32).reshape(8, 8, 8, 128)

    def across(v):
        return v + jnp.where(even, pltpu.roll(v, 120, 1), pltpu.roll(v, 8, 1))

    mean = across(jnp.sum(jnp.sum(tri, axis=0), axis=1)) * (1.0 / 128)
    center = tri - mean[None, :, None, :]
    spread = across(jnp.sum(jnp.sum(center * center, axis=0), axis=1)) * (1.0 / 128)
    inverse = lax.rsqrt(spread + EPS)
    e_f[0:128, :] = pm[...].reshape(128, 128)
    g_e = e_f[pl.ds(0, 64, stride=2), :]
    g_o = e_f[pl.ds(1, 64, stride=2), :]
    gain = jnp.where(even, g_e[:, 2:3], g_o[:, 2:3])
    bias = jnp.where(even, g_e[:, 3:4], g_o[:, 3:4])
    hidden = jnp.concatenate(
        [
            (center[:, r].reshape(64, 128) * inverse[r:r + 1] * gain + bias).astype(BF16)
            for r in range(8)
        ],
        axis=1,
    )
    both = dot(wot[...], hidden)
    for q in range(4):
        a0 = both[0:128, 256 * q:256 * q + 128]
        a1 = both[0:128, 256 * q + 128:256 * q + 256]
        b0 = both[128:256, 256 * q:256 * q + 128]
        b1 = both[128:256, 256 * q + 128:256 * q + 256]
        mixed = jnp.where(even, a0 + pltpu.roll(b0, 120, 1), b1 + pltpu.roll(a1, 8, 1))
        fs[:, q] = mixed.astype(BF16).reshape(8, 16, 128)

    def f_copy():
        return pltpu.make_async_remote_copy(
            src_ref=fs.at[chan], dst_ref=fr.at[me_m], send_sem=fs_sem.at[0], recv_sem=fr_sem.at[me_m],
            device_id=(row_f, chan), device_id_type=MESH,
        )

    for s in range(1, NCH):
        c = lax.rem(chan + s, NCH)
        send(fs.at[c], fr.at[me_m], fs_sem.at[s], fr_sem.at[me_m], row_f, c)

    @pl.when(jnp.logical_not(self_f))
    def _():
        f_copy().start()

    @pl.when(self_f)
    def _():
        fr[me_m] = fs[chan]

    drain(NCH - 1)

    def finish(z):
        got = jnp.concatenate([fr[z * NX + i].reshape(64, 128) for i in range(NX)], axis=1)
        o = dot(got, perm[...])
        for q in range(4):
            for par in range(2):
                r = 2 * q + par
                for half in range(2):
                    val = o[16 * q:16 * q + 16, 256 * par + 128 * half:256 * par + 128 * half + 128]
                    o_f[2 * z + half, pl.ds(r, 16, stride=8), :] = val * gate[2 * z + half, r]

    for s in range(1, NX):
        m = zh * NX + lax.rem(x + s, NX)
        arrived(fr.at[m], fs_sem.at[s], fr_sem.at[m])

    @pl.when(jnp.logical_not(self_f))
    def _():
        arrived(fr.at[me_m], fs_sem.at[0], fr_sem.at[me_m])

    finish(zh)
    for i in range(NX):
        m = (1 - zh) * NX + i
        arrived(fr.at[m], fs_sem.at[NX + i], fr_sem.at[m])
    finish(1 - zh)
    for n in range(4):
        out[:, :, 128 * n:128 * n + 128] = o_f[n].reshape(16, 8, 128).astype(BF16)

    drain(0)

    @pl.when(jnp.logical_not(self_f))
    def _():
        f_copy().wait_send()


def body(pair_in, token_mask, in_gain, in_bias, in_weight, out_gain, out_bias, out_weight, gate_weight):
    vm = pl.BlockSpec(memory_space=pltpu.VMEM)
    dma = pltpu.SemaphoreType.DMA
    return pl.pallas_call(
        kernel,
        out_shape=pltpu.VMEM((16, 8, 512), BF16),
        in_specs=[pl.BlockSpec(memory_space=pltpu.HBM)] * 10,
        out_specs=vm,
        scratch_shapes=[
            pltpu.VMEM((16, 8, 512), BF16),
            pltpu.VMEM((1, 16), BF16),
            pltpu.VMEM((1, 16), BF16),
            pltpu.VMEM((1, 16), F32),
            pltpu.VMEM((1, 16), F32),
            pltpu.VMEM((1, 512), jnp.int32),
            pltpu.VMEM((4, 16, 128), BF16),
            pltpu.VMEM((128, 128), BF16),
            pltpu.VMEM((16, 128), BF16),
            pltpu.SMEM((512,), jnp.int32),
            dma((10,)),
            pltpu.VMEM((T, 128, KC), F32),
            pltpu.VMEM((T, NCH, 8, 16, KC), BF16),
            pltpu.VMEM((NCH, 16, 128), F32),
            pltpu.VMEM((2, 128, 128), F32),
            pltpu.VMEM((2, 128, KC), F32),
            pltpu.VMEM((T, 8, 128, KC), BF16),
            pltpu.VMEM((T, 8, 128, KC), BF16),
            pltpu.VMEM((8, 128, 128), F32),
            pltpu.VMEM((512, 128), F32),
            pltpu.VMEM((8, 64, 128), BF16),
            pltpu.VMEM((8, 64, 128), BF16),
            pltpu.VMEM((8, 4, 16, 128), BF16),
            pltpu.VMEM((8, 4, 16, 128), BF16),
            pltpu.VMEM((T, 8, 16, KC), F32),
            pltpu.VMEM((512, 512), BF16),
            pltpu.VMEM((256, 64), BF16),
            pltpu.VMEM((4, 128, 128), F32),
            dma((T, 8)), dma((T, NCH)),
            dma((NCH,)), dma((NCH,)),
            dma((T, 7)), dma((T, 8)),
            dma((T, 7)), dma((T, 8)),
            dma((NCH,)), dma((NCH,)),
            dma((NCH,)), dma((NCH,)),
        ],
        compiler_params=pltpu.CompilerParams(
            collective_id=0, has_side_effects=True, vmem_limit_bytes=60 * 1024 * 1024
        ),
    )(
        pair_in,
        in_gain.reshape(1, 16),
        in_bias.reshape(1, 16),
        out_gain.reshape(1, 16),
        out_bias.reshape(1, 16),
        token_mask.reshape(1, 512),
        jnp.transpose(in_weight, (0, 2, 1)),
        out_weight,
        gate_weight.T,
        token_mask,
    )


def solution(mesh):
    return jax.shard_map(
        body,
        mesh=mesh,
        in_specs=(
            P("chan", "row", None),
            P(),
            P("chan"),
            P("chan"),
            P(None, None, "chan"),
            P("chan"),
            P("chan"),
            P(),
            P(None, "chan"),
        ),
        out_specs=P("chan", "row", None),
        check_vma=False,
    )
```

```python
import jax
import jax.numpy as jnp
from jax import lax
from jax.experimental import pallas as pl
from jax.experimental.pallas import tpu as pltpu
from jax.sharding import PartitionSpec as P

MESH = pl.DeviceIdType.MESH
EPS = 1e-05
NZH, NY, NX, NZL, NC = 2, 8, 4, 4, 2
NCH = NZL * NC
T = 4
KC = 128
AHEAD = 2
ORDER = (
    ("relay", 0), ("send", 2), ("relay", 1), ("par", 0), ("in", 0), ("send", 3), ("proj", 0), ("s1", 0), ("relay", 2),
    ("in", 1), ("proj", 1), ("s1", 1), ("relay", 3), ("s2", 0),
    ("in", 2), ("proj", 2), ("s1", 2), ("s2l", 0), ("s2", 1),
    ("in", 3), ("proj", 3), ("s1", 3), ("s2l", 1), ("s2", 2), ("s2l", 2), ("s2", 3), ("s3", 0), ("s2l", 3),
    ("s3", 1), ("s3", 2), ("s3", 3),
)
F32 = jnp.float32
BF16 = jnp.bfloat16


def dot(a, b):
    return jnp.dot(a, b, preferred_element_type=F32)


def column(vec):
    n = vec.shape[1]
    a = lax.broadcasted_iota(jnp.int32, (n, n), 0)
    b = lax.broadcasted_iota(jnp.int32, (n, n), 1)
    return jnp.sum(jnp.where(a == b, jnp.broadcast_to(vec, (n, n)), 0.0), axis=1, keepdims=True)


def kernel(
    *refs,
):
    ins, (out, *vins), (sem_in, *rest) = refs[:10], refs[10:21], refs[21:]
    run(ins, out, vins, sem_in, *rest)


def run(
    ins, out, vins, sem_in,
    xf, xb, pm, gb, lr_f, lb, rb, acc, e_f, es, er, fs, fr, gate, perm, wot, o_f,
    xs_sem, xr_sem, ps_sem, pr_sem, ls_sem, lr_sem, rs_sem, rr_sem, es_sem, er_sem, fs_sem, fr_sem,
):
    loads = [pltpu.make_async_copy(a, b, sem_in.at[n]) for n, (a, b) in enumerate(zip(ins, vins))]
    for load in loads:
        load.start()
    pair, ig, ib, og, ob, tm_v, w, wo, gw, tm_s = vins
    row = lax.axis_index("row")
    chan = lax.axis_index("chan")
    zh = lax.div(row, NY * NX)
    y = lax.rem(lax.div(row, NX), NY)
    x = lax.rem(row, NX)
    zl = lax.div(chan, NC)
    core = lax.rem(chan, NC)
    me_m = zh * NX + x

    def row_of(zh_, y_, x_):
        return (zh_ * NY + y_) * NX + x_

    def yrow(d):
        return row_of(zh, lax.rem(y + (NY + d), NY), x)

    def xrow(d):
        return row_of(zh, y, lax.rem(x + (NX + d), NX))

    row_z = row_of(1 - zh, y, x)
    row_f = row_of(lax.div(chan, NX), y, lax.rem(chan, NX))
    self_f = me_m == chan
    sibling = zl * NC + (1 - core)
    z_two = lax.rem(zl + 2, NZL)
    z_pair = zl + 1 - 2 * lax.rem(zl, 2)
    z_inner = NZL - 1 - zl
    inner = jnp.logical_and(zl > 0, zl < NZL - 1)

    bar = pltpu.get_barrier_semaphore()

    def greet(r, c):
        pl.semaphore_signal(bar, inc=1, device_id=(r, c), device_id_type=MESH)

    for s in range(1, NCH):
        greet(row, lax.rem(chan + s, NCH))
    for r in (yrow(2), yrow(-2), xrow(2), yrow(1), yrow(-1), xrow(1), xrow(-1)):
        greet(r, chan)
    at_z = 4 * zh + zl + jnp.where(zl < 2, 7 - zl, 12 - zl)
    greet(row_of(lax.rem(lax.div(at_z, NZL), NZH), y, x), lax.rem(at_z, NZL) * NC + core)

    sends = []

    def send(src, dst, ssem, rsem, r, c, when=None):
        copy = pltpu.make_async_remote_copy(
            src_ref=src, dst_ref=dst, send_sem=ssem, recv_sem=rsem,
            device_id=(r, c), device_id_type=MESH,
        )
        if when is None:
            copy.start()
        else:
            pl.when(when)(copy.start)
        sends.append((copy, when))

    def drain(keep):
        while len(sends) > keep:
            copy, when = sends.pop(0)
            if when is None:
                copy.wait_send()
            else:
                pl.when(when)(copy.wait_send)

    def arrived(ref, ssem, rsem):
        pltpu.make_async_remote_copy(
            src_ref=ref, dst_ref=ref, send_sem=ssem, recv_sem=rsem,
            device_id=(row, sibling), device_id_type=MESH,
        ).wait_recv()

    def prepare(t):
        xf[t] = pair[:, :, t * KC:(t + 1) * KC].astype(F32).reshape(128, KC)
        for r in range(8):
            xb[t, chan, r] = xf[t, pl.ds(r, 16, stride=8), :].astype(BF16)

    def send_in(t):
        for n, (z, when) in enumerate(((z_two, None), (z_inner, inner), (z_pair, None))):
            send(xb.at[t, chan], xb.at[t, chan], xs_sem.at[t, 1 + n], xr_sem.at[t, chan], row, z * NC + core, when)
        send(xb.at[t, chan], xb.at[t, chan], xs_sem.at[t, 0], xr_sem.at[t, chan], row, sibling)

    for load in loads[1:5]:
        load.wait()
    lane16 = lax.broadcasted_iota(jnp.int32, (16, 128), 1)
    cols = [column(v[...].astype(F32)) for v in (ig, ib, og, ob)]
    block = jnp.zeros((16, 128), F32)
    for n, col in enumerate(cols):
        block = jnp.where(lane16 == n, jnp.broadcast_to(col, (16, 128)), block)
    pm[chan] = block
    loads[0].wait()
    prepare(0)
    pl.semaphore_wait(bar, jnp.where(inner, NCH - 1 + 7, NCH - 1 + 7 + 2))
    for s in range(1, NCH):
        send(pm.at[chan], pm.at[chan], ps_sem.at[s], pr_sem.at[chan], row, lax.rem(chan + s, NCH))
    send_in(0)
    for t in range(1, AHEAD):
        prepare(t)
        send_in(t)

    for t in range(AHEAD, T):
        prepare(t)

    for load in loads[5:]:
        load.wait()

    ki = lax.broadcasted_iota(jnp.int32, (512, 512), 0)
    ni = lax.broadcasted_iota(jnp.int32, (512, 512), 1)
    kx, ky, kp, k8 = ki >> 7, (ki >> 4) & 7, (ki >> 3) & 1, ki & 7
    want = (kp << 8) | (ky << 5) | (kx << 3) | k8
    perm[...] = jnp.where(want == ni, 1.0, 0.0).astype(BF16)
    eye_a = lax.broadcasted_iota(jnp.int32, (128, 128), 0)
    eye_b = lax.broadcasted_iota(jnp.int32, (128, 128), 1)
    eye = jnp.where(eye_a == eye_b, 1.0, 0.0).astype(BF16)
    turned = lax.dot_general(eye, wo[...], (((1,), (1,)), ((), ())), preferred_element_type=F32).astype(BF16)
    ha = lax.broadcasted_iota(jnp.int32, (128, 64), 0)
    hb = lax.broadcasted_iota(jnp.int32, (128, 64), 1)
    for par in range(2):
        pick = jnp.where(ha == 2 * hb + par, 1.0, 0.0).astype(BF16)
        wot[par * 128:(par + 1) * 128, :] = dot(turned, pick).astype(BF16)

    wt = jnp.concatenate([w[...].reshape(64, 128), gw[...]], axis=0)

    def params(t):
        for s in range(1, NCH):
            c = lax.rem(chan + s, NCH)
            arrived(pm.at[c], ps_sem.at[s], pr_sem.at[c])
        for n in range(2):
            gb[n] = jnp.broadcast_to(pm[...].reshape(128, 128)[:, n:n + 1], (128, 128))

    row_valid = [tm_s[row * 8 + r].astype(F32) for r in range(8)]

    early = []

    def relay(t):
        c = z_two * NC + core
        arrived(xb.at[t, c], xs_sem.at[t, 0], xr_sem.at[t, c])
        send(xb.at[t, c], xb.at[t, c], xs_sem.at[t, 4], xr_sem.at[t, c], row, z_pair * NC + core, inner)
        early.append(t)

    def gather_in(t):
        for n, z in enumerate((z_two, z_pair, z_inner)):
            c = z * NC + core
            if t not in early or n != 0:
                arrived(xb.at[t, c], xs_sem.at[t, 0], xr_sem.at[t, c])
            if n == 0 and t not in early:
                send(xb.at[t, c], xb.at[t, c], xs_sem.at[t, 4], xr_sem.at[t, c], row, z_pair * NC + core, inner)
            send(xb.at[t, c], xb.at[t, c], xs_sem.at[t, 5 + n], xr_sem.at[t, c], row, sibling)
        for d in range(NZL):
            c = lax.rem(zl + d, NZL) * NC + (1 - core)
            arrived(xb.at[t, c], xs_sem.at[t, 0], xr_sem.at[t, c])

    def project(t):
        pieces = []
        gain = gb[0]
        bias = gb[1]
        for r in range(8):
            v = xb[t, :, r].astype(F32).reshape(128, KC)
            mean = jnp.sum(v, axis=0, keepdims=True) * (1.0 / 128)
            center = v - mean
            spread = jnp.sum(center * center, axis=0, keepdims=True) * (1.0 / 128)
            pieces.append((center * lax.rsqrt(spread + EPS) * gain + bias).astype(BF16))
        normed = jnp.concatenate(pieces, axis=1)
        proj = dot(wt, normed)
        col_valid = tm_v[:, t * KC:(t + 1) * KC].astype(F32)
        mask = jnp.concatenate([col_valid * s for s in row_valid], axis=1)
        left = jax.nn.sigmoid(proj[16:32]) * proj[0:16] * mask
        right = jax.nn.sigmoid(proj[48:64]) * proj[32:48] * mask
        g = jax.nn.sigmoid(proj[64:80])
        for r in range(8):
            lr_f[0, pl.ds(r, 16, stride=8), :] = left[:, r * KC:(r + 1) * KC]
            lr_f[1, pl.ds(r, 16, stride=8), :] = right[:, r * KC:(r + 1) * KC]
            gate[t, r] = g[:, r * KC:(r + 1) * KC]
        lb[t, me_m] = lr_f[0].astype(BF16)
        rb[t, y] = lr_f[1].astype(BF16)

    def lslot(far, d):
        return (1 - zh if far else zh) * NX + lax.rem(x + (NX + d), NX)

    def rslot(d):
        return lax.rem(y + (NY + d), NY)

    def send_l(t, n, slot, r):
        send(lb.at[t, slot], lb.at[t, slot], ls_sem.at[t, n], lr_sem.at[t, slot], r, chan)

    def send_r(t, n, slot, r):
        send(rb.at[t, slot], rb.at[t, slot], rs_sem.at[t, n], rr_sem.at[t, slot], r, chan)

    def got_l(t, slot):
        arrived(lb.at[t, slot], ls_sem.at[t, 0], lr_sem.at[t, slot])

    def got_r(t, slot):
        arrived(rb.at[t, slot], rs_sem.at[t, 0], rr_sem.at[t, slot])

    def step1(t):
        send_l(t, 0, me_m, row_z)
        send_r(t, 0, y, yrow(2))
        send_r(t, 1, y, yrow(-2))
        send_r(t, 2, y, yrow(1))
        send_r(t, 3, y, yrow(-1))
        send_l(t, 1, me_m, xrow(2))
        send_l(t, 2, me_m, xrow(1))
        send_l(t, 3, me_m, xrow(-1))

    def step2(t):
        got_r(t, rslot(-2))
        if t % 2 == 0:
            send_r(t, 6, rslot(-2), yrow(2))
        send_r(t, 4, rslot(-2), yrow(1))
        got_r(t, rslot(2))
        if t % 2 == 1:
            send_r(t, 6, rslot(2), yrow(-2))
        send_r(t, 5, rslot(2), yrow(-1))

    def step2l(t):
        got_l(t, lslot(True, 0))
        send_l(t, 4, lslot(True, 0), xrow(2))
        send_l(t, 5, lslot(True, 0), xrow(1))
        send_l(t, 6, lslot(True, 0), xrow(-1))

    def step3(t):
        for d in (-1, 1, 2):
            got_l(t, lslot(False, d))
            got_l(t, lslot(True, d))
        for d in (-1, 1, -3, 3, 4):
            got_r(t, rslot(d))
        for h in range(8):
            a = lb[t, :, 16 * h:16 * h + 16, :].reshape(128, KC)
            b = rb[t, :, 16 * h:16 * h + 16, :].reshape(128, KC)
            part = lax.dot_general(a, b, (((1,), (1,)), ((), ())), preferred_element_type=F32)
            if t == 0:
                acc[h] = part
            else:
                acc[h] += part

    for step, t in ORDER:
        {"in": gather_in, "send": send_in, "relay": relay, "par": params, "proj": project, "s1": step1, "s2": step2, "s2l": step2l, "s3": step3}[step](t)

    lane = lax.broadcasted_iota(jnp.int32, (1, 128), 1)
    even = ((lane >> 3) & 1) == 0

    for h in range(8):
        o = acc[h].reshape(8, 2, 8, 128)
        own = jnp.where(even, o[:, 0].reshape(64, 128), o[:, 1].reshape(64, 128))
        e_f[pl.ds(h, 64, stride=8), :] = own
    es[...] = e_f[...].astype(BF16).reshape(8, 64, 128)
    for s in range(1, NCH):
        c = lax.rem(chan + s, NCH)
        send(es.at[c], er.at[chan], es_sem.at[s], er_sem.at[chan], row, c)
    er[chan] = es[chan]
    drain(NCH - 1)
    for s in range(1, NCH):
        c = lax.rem(chan + s, NCH)
        arrived(er.at[c], es_sem.at[s], er_sem.at[c])

    tri = er[...].astype(F32).reshape(8, 8, 8, 128)

    def across(v):
        return v + jnp.where(even, pltpu.roll(v, 120, 1), pltpu.roll(v, 8, 1))

    mean = across(jnp.sum(jnp.sum(tri, axis=0), axis=1)) * (1.0 / 128)
    center = tri - mean[None, :, None, :]
    spread = across(jnp.sum(jnp.sum(center * center, axis=0), axis=1)) * (1.0 / 128)
    inverse = lax.rsqrt(spread + EPS)
    e_f[0:128, :] = pm[...].reshape(128, 128)
    g_e = e_f[pl.ds(0, 64, stride=2), :]
    g_o = e_f[pl.ds(1, 64, stride=2), :]
    gain = jnp.where(even, g_e[:, 2:3], g_o[:, 2:3])
    bias = jnp.where(even, g_e[:, 3:4], g_o[:, 3:4])
    hidden = jnp.concatenate(
        [
            (center[:, r].reshape(64, 128) * inverse[r:r + 1] * gain + bias).astype(BF16)
            for r in range(8)
        ],
        axis=1,
    )
    both = dot(wot[...], hidden)
    for q in range(4):
        a0 = both[0:128, 256 * q:256 * q + 128]
        a1 = both[0:128, 256 * q + 128:256 * q + 256]
        b0 = both[128:256, 256 * q:256 * q + 128]
        b1 = both[128:256, 256 * q + 128:256 * q + 256]
        mixed = jnp.where(even, a0 + pltpu.roll(b0, 120, 1), b1 + pltpu.roll(a1, 8, 1))
        fs[:, q] = mixed.astype(BF16).reshape(8, 16, 128)

    def f_copy():
        return pltpu.make_async_remote_copy(
            src_ref=fs.at[chan], dst_ref=fr.at[me_m], send_sem=fs_sem.at[0], recv_sem=fr_sem.at[me_m],
            device_id=(row_f, chan), device_id_type=MESH,
        )

    for s in range(1, NCH):
        c = lax.rem(chan + s, NCH)
        send(fs.at[c], fr.at[me_m], fs_sem.at[s], fr_sem.at[me_m], row_f, c)

    @pl.when(jnp.logical_not(self_f))
    def _():
        f_copy().start()

    @pl.when(self_f)
    def _():
        fr[me_m] = fs[chan]

    drain(NCH - 1)

    def finish(z):
        got = jnp.concatenate([fr[z * NX + i].reshape(64, 128) for i in range(NX)], axis=1)
        o = dot(got, perm[...])
        for q in range(4):
            for par in range(2):
                r = 2 * q + par
                for half in range(2):
                    val = o[16 * q:16 * q + 16, 256 * par + 128 * half:256 * par + 128 * half + 128]
                    o_f[2 * z + half, pl.ds(r, 16, stride=8), :] = val * gate[2 * z + half, r]

    for s in range(1, NX):
        m = zh * NX + lax.rem(x + s, NX)
        arrived(fr.at[m], fs_sem.at[s], fr_sem.at[m])

    @pl.when(jnp.logical_not(self_f))
    def _():
        arrived(fr.at[me_m], fs_sem.at[0], fr_sem.at[me_m])

    finish(zh)
    for i in range(NX):
        m = (1 - zh) * NX + i
        arrived(fr.at[m], fs_sem.at[NX + i], fr_sem.at[m])
    finish(1 - zh)
    for n in range(4):
        out[:, :, 128 * n:128 * n + 128] = o_f[n].reshape(16, 8, 128).astype(BF16)

    drain(0)

    @pl.when(jnp.logical_not(self_f))
    def _():
        f_copy().wait_send()


def body(pair_in, token_mask, in_gain, in_bias, in_weight, out_gain, out_bias, out_weight, gate_weight):
    vm = pl.BlockSpec(memory_space=pltpu.VMEM)
    dma = pltpu.SemaphoreType.DMA
    return pl.pallas_call(
        kernel,
        out_shape=pltpu.VMEM((16, 8, 512), BF16),
        in_specs=[pl.BlockSpec(memory_space=pltpu.HBM)] * 10,
        out_specs=vm,
        scratch_shapes=[
            pltpu.VMEM((16, 8, 512), BF16),
            pltpu.VMEM((1, 16), BF16),
            pltpu.VMEM((1, 16), BF16),
            pltpu.VMEM((1, 16), F32),
            pltpu.VMEM((1, 16), F32),
            pltpu.VMEM((1, 512), jnp.int32),
            pltpu.VMEM((4, 16, 128), BF16),
            pltpu.VMEM((128, 128), BF16),
            pltpu.VMEM((16, 128), BF16),
            pltpu.SMEM((512,), jnp.int32),
            dma((10,)),
            pltpu.VMEM((T, 128, KC), F32),
            pltpu.VMEM((T, NCH, 8, 16, KC), BF16),
            pltpu.VMEM((NCH, 16, 128), F32),
            pltpu.VMEM((2, 128, 128), F32),
            pltpu.VMEM((2, 128, KC), F32),
            pltpu.VMEM((T, 8, 128, KC), BF16),
            pltpu.VMEM((T, 8, 128, KC), BF16),
            pltpu.VMEM((8, 128, 128), F32),
            pltpu.VMEM((512, 128), F32),
            pltpu.VMEM((8, 64, 128), BF16),
            pltpu.VMEM((8, 64, 128), BF16),
            pltpu.VMEM((8, 4, 16, 128), BF16),
            pltpu.VMEM((8, 4, 16, 128), BF16),
            pltpu.VMEM((T, 8, 16, KC), F32),
            pltpu.VMEM((512, 512), BF16),
            pltpu.VMEM((256, 64), BF16),
            pltpu.VMEM((4, 128, 128), F32),
            dma((T, 8)), dma((T, NCH)),
            dma((NCH,)), dma((NCH,)),
            dma((T, 7)), dma((T, 8)),
            dma((T, 7)), dma((T, 8)),
            dma((NCH,)), dma((NCH,)),
            dma((NCH,)), dma((NCH,)),
        ],
        compiler_params=pltpu.CompilerParams(
            collective_id=0, has_side_effects=True, vmem_limit_bytes=60 * 1024 * 1024
        ),
    )(
        pair_in,
        in_gain.reshape(1, 16),
        in_bias.reshape(1, 16),
        out_gain.reshape(1, 16),
        out_bias.reshape(1, 16),
        token_mask.reshape(1, 512),
        jnp.transpose(in_weight, (0, 2, 1)),
        out_weight,
        gate_weight.T,
        token_mask,
    )


def solution(mesh):
    return jax.shard_map(
        body,
        mesh=mesh,
        in_specs=(
            P("chan", "row", None),
            P(),
            P("chan"),
            P("chan"),
            P(None, None, "chan"),
            P("chan"),
            P("chan"),
            P(),
            P(None, "chan"),
        ),
        out_specs=P("chan", "row", None),
        check_vma=False,
    )
```
